32 devices in a mesh: dp: 8 (over z, core), tensor: 4 (over y, x).
Axes of the slice: x: 2, y: 2, z: 4, core: 2. Of those that a mesh axis runs over, the one named last changes fastest.
Arguments:
- teacher_queries: bfloat16 [8, 512, 8192], P('dp', None, 'tensor'), may hold values from -100 to 100
- teacher_keys: bfloat16 [8, 512, 1024], P('dp', None, 'tensor'), may hold values from -5 to 5
- teacher_values: bfloat16 [8, 512, 1024], P('dp', None, 'tensor'), may hold values from -6 to 6
- projector: bfloat16 [8192, 4096], P('tensor'), may hold values from -0.25 to 0.25
- student_inputs: bfloat16 [8, 512, 4096], P('dp', 'tensor'), may hold values from -30 to 30
- query_weight: bfloat16 [4096, 4096], P('dp', 'tensor'), may hold values from -1 to 1
- key_weight: bfloat16 [4096, 1024], P('dp', 'tensor'), may hold values from -1 to 1
- value_weight: bfloat16 [4096, 1024], P('dp', 'tensor'), may hold values from -0.09375 to 0.09375
Outputs:
- query_grad: float32 [4096, 4096], P('dp', 'tensor')
- key_grad: float32 [4096, 1024], P('dp', 'tensor')
- value_grad: float32 [4096, 1024], P('dp', 'tensor')
The draws below stay inside these ranges and needn't reach their ends.
All inputs are finite; a program needn't handle non-finite values.
Results may differ from the reference program's by a relative error of at most 0.029.
Values may be sent and summed in bfloat16 or wider, within the bound.
A program may use at most 128 MiB of HBM per device.

```python
import jax
import jax.numpy as jnp
from jax import lax

TDIM = 8192
SDIM = 4096
HEAD = 128
TQH = 64
TKVH = 8
SQH = 32
SKVH = 8
SEQ = 512
N_DP = 8
N_TENSOR = 4


def shared_keys(key):
    keys = jax.random.truncated_normal(key, -5.0, 5.0, (N_DP, SEQ, TKVH * HEAD), jnp.float32)
    position = jnp.arange(SEQ)[None, :, None]
    following = jnp.roll(keys, -1, axis=1)
    return jnp.where(position % 16 == 13, 0.985 * following, keys)


def student_pairs(key):
    inner = jax.random.fold_in(key, 21)
    scale = (SDIM // 4) ** (-0.5)
    return jax.random.truncated_normal(inner, -4.0, 4.0, (SDIM, SKVH * HEAD), jnp.float32) * scale


def draw_teacher_keys(key, part):
    base = shared_keys(key)
    return base.astype(jnp.bfloat16)


def draw_teacher_queries(key, part):
    key = jax.random.fold_in(key, 7)
    queries = jax.random.truncated_normal(key, -5.0, 5.0, (N_DP, SEQ, TDIM), jnp.float32)
    return queries.astype(jnp.bfloat16)


def draw_key_weight(key, part):
    base = student_pairs(key)
    return base.astype(jnp.bfloat16)


def draw_query_weight(key, part):
    key = jax.random.fold_in(key, 17)
    scale = (SDIM // 4) ** (-0.5)
    weights = jax.random.truncated_normal(key, -4.0, 4.0, (SDIM, SDIM), jnp.float32) * scale
    return weights.astype(jnp.bfloat16)


def draw_student_inputs(key, part):
    key = jax.random.fold_in(key, 9)
    normal_key, order_key = jax.random.split(key, 2)
    rows = jax.random.truncated_normal(normal_key, -4.0, 4.0, (N_DP, SEQ, SDIM), jnp.float32)
    paired = jax.random.permutation(order_key, N_DP)
    block = jnp.arange(SDIM) // (SDIM // N_DP)
    spike = jnp.where(block[None, None, :] == paired[:, None, None], 3.0, 1.0)
    rows = rows * spike
    return rows.astype(jnp.bfloat16)


def level_of(key, dims, shards, smallest, largest):
    loudness, own = 1.0, jax.random.fold_in(key, 6)
    for dim, shards_of in shards:
        draws = jnp.exp(jax.random.uniform(jax.random.fold_in(own, dim), (shards_of,), jnp.float32, smallest / len(shards), largest / len(shards)))
        loudness = loudness * jnp.repeat(draws, dims[dim] // shards_of).reshape([-1 if axis == dim else 1 for axis in range(len(dims))])
    return loudness


def normal_values(own_key, dims, scale, bound, cuts=(), dtype=jnp.bfloat16):
    loudness = level_of(own_key, dims, cuts, -0.22, 0.18) if cuts else 1.0
    values = jax.random.normal(own_key, dims, jnp.float32) * scale * loudness
    return jnp.minimum(jnp.maximum(values, -bound), bound).astype(dtype)


def setup_inputs(seed: int = 0) -> dict:
    seeds = jax.random.split(jax.random.key(seed), 9)
    teacher_queries = draw_teacher_queries(jax.random.fold_in(seeds[8], 71), 0)
    teacher_keys = draw_teacher_keys(jax.random.fold_in(seeds[8], 71), 0)
    teacher_values = normal_values(seeds[2], (N_DP, SEQ, TKVH * HEAD), 1.0, 6.0, ((0, 8), (2, 4)))
    projector = normal_values(seeds[3], (TDIM, SDIM), (TDIM // 16) ** -0.5, 0.25, ((0, 4),))
    student_inputs = draw_student_inputs(jax.random.fold_in(seeds[8], 71), 0)
    query_weight = draw_query_weight(jax.random.fold_in(seeds[8], 71), 0)
    key_weight = draw_key_weight(jax.random.fold_in(seeds[8], 71), 0)
    value_weight = normal_values(seeds[7], (SDIM, SKVH * HEAD), SDIM ** -0.5, 0.09375, ((0, 8), (1, 4)))
    return dict(teacher_queries=teacher_queries, teacher_keys=teacher_keys, teacher_values=teacher_values, projector=projector, student_inputs=student_inputs, query_weight=query_weight, key_weight=key_weight, value_weight=value_weight)


def attend(queries, keys, values, groups, factor):
    length = queries.shape[0]
    heads_kv = keys.shape[1] // HEAD
    query_heads = queries.astype(jnp.float32).reshape(length, heads_kv, groups, HEAD)
    key_heads = keys.astype(jnp.float32).reshape(length, heads_kv, HEAD)
    value_heads = values.astype(jnp.float32).reshape(length, heads_kv, HEAD)
    block_rows = min(512, length)
    pieces = []
    kept = []
    for number in range(length // block_rows):
        first = number * block_rows
        limit = first + block_rows
        scores = jnp.einsum("qhgd,khd->hgqk", query_heads[first:limit], key_heads[:limit]) * factor
        visible = jnp.arange(limit)[None, :] <= (first + jnp.arange(block_rows))[:, None]
        scores = jnp.where(visible, scores, -1e30)
        shifted = jnp.exp(scores - jnp.max(scores, axis=-1, keepdims=True))
        probs = shifted / jnp.sum(shifted, axis=-1, keepdims=True)
        rounded = lax.optimization_barrier(probs.astype(jnp.bfloat16)).astype(jnp.float32)
        context = jnp.einsum("hgqk,khd->qhgd", rounded, value_heads[:limit])
        pieces.append(context.reshape(block_rows, -1))
        kept.append(probs)
    return jnp.concatenate(pieces, axis=0), kept


def attend_back(incoming_all, queries, keys, values, kept, groups, factor):
    length = queries.shape[0]
    heads_kv = keys.shape[1] // HEAD
    query_heads = queries.astype(jnp.float32).reshape(length, heads_kv, groups, HEAD)
    key_heads = keys.astype(jnp.float32).reshape(length, heads_kv, HEAD)
    value_heads = values.astype(jnp.float32).reshape(length, heads_kv, HEAD)
    block_rows = min(512, length)
    grad_keys = jnp.zeros((length, heads_kv, HEAD), jnp.float32)
    grad_values = jnp.zeros((length, heads_kv, HEAD), jnp.float32)
    query_parts = []
    for number in range(length // block_rows):
        first = number * block_rows
        limit = first + block_rows
        probs = kept[number]
        rounded = lax.optimization_barrier(probs.astype(jnp.bfloat16)).astype(jnp.float32)
        incoming = incoming_all[first:limit].astype(jnp.float32).reshape(block_rows, heads_kv, groups, HEAD)
        grad_values = grad_values.at[:limit].add(jnp.einsum("hgqk,qhgd->khd", rounded, incoming))
        grad_probs = jnp.einsum("qhgd,khd->hgqk", incoming, value_heads[:limit])
        grad_scores = probs * (grad_probs - jnp.sum(grad_probs * probs, axis=-1, keepdims=True))
        scaled = lax.optimization_barrier((grad_scores * factor).astype(jnp.bfloat16)).astype(jnp.float32)
        query_parts.append(jnp.einsum("hgqk,khd->qhgd", scaled, key_heads[:limit]).reshape(block_rows, -1))
        grad_keys = grad_keys.at[:limit].add(jnp.einsum("hgqk,qhgd->khd", scaled, query_heads[first:limit]))
    grad_queries = jnp.concatenate(query_parts, axis=0).astype(jnp.bfloat16)
    return grad_queries, grad_keys.reshape(length, -1).astype(jnp.bfloat16), grad_values.reshape(length, -1).astype(jnp.bfloat16)


def reference(teacher_queries, teacher_keys, teacher_values, projector, student_inputs, query_weight, key_weight, value_weight):
    factor = HEAD ** -0.5
    width = TDIM // N_TENSOR
    weights = jnp.concatenate([query_weight, key_weight, value_weight], axis=1)
    kv_cols = SKVH * HEAD

    def one_sequence(carry, number):
        context_t, unused = attend(teacher_queries[number], teacher_keys[number], teacher_values[number], TQH // TKVH, factor)
        context_t = context_t.astype(jnp.bfloat16)
        target = jnp.zeros((SEQ, SDIM), jnp.float32)
        for block in range(N_TENSOR):
            partial_sum = jnp.dot(context_t[:, block * width:(block + 1) * width], projector[block * width:(block + 1) * width], preferred_element_type=jnp.float32)
            target = target + lax.optimization_barrier(partial_sum.astype(jnp.bfloat16)).astype(jnp.float32)
        inputs = student_inputs[number]
        projected = jnp.dot(inputs, weights, preferred_element_type=jnp.float32).astype(jnp.bfloat16)
        queries = projected[:, :SDIM]
        keys = projected[:, SDIM:SDIM + kv_cols]
        values = projected[:, SDIM + kv_cols:]
        context_s, kept = attend(queries, keys, values, SQH // SKVH, factor)
        grad_context = ((context_s - target) / N_DP).astype(jnp.bfloat16)
        grad_q, grad_k, grad_v = attend_back(grad_context, queries, keys, values, kept, SQH // SKVH, factor)
        grad_all = jnp.concatenate([grad_q, grad_k, grad_v], axis=1)
        term = jnp.dot(inputs.astype(jnp.float32).T, grad_all.astype(jnp.float32))
        return carry + term, 0

    start = jnp.zeros((SDIM, SDIM + 2 * kv_cols), jnp.float32)
    total, unused = lax.scan(one_sequence, start, jnp.arange(N_DP))
    return total[:, :SDIM], total[:, SDIM:SDIM + kv_cols], total[:, SDIM + kv_cols:]
```

```python
import functools

import jax
import jax.numpy as jnp
from jax import lax
from jax.experimental import pallas as pl
from jax.experimental.pallas import tpu as pltpu
from jax.sharding import PartitionSpec as P

HEAD = 128
TQH = 64
TKVH = 8
SQH = 32
SKVH = 8
VMEM_LIMIT = 63 * 1024 * 1024


def attend(queries, keys, values, groups, factor):
    length = queries.shape[0]
    heads_kv = keys.shape[1] // HEAD
    query_heads = queries.reshape(length, heads_kv, groups, HEAD)
    key_heads = keys.reshape(length, heads_kv, HEAD)
    value_heads = values.reshape(length, heads_kv, HEAD)
    block_rows = min(512, length)
    pieces = []
    kept = []
    for number in range(length // block_rows):
        first = number * block_rows
        limit = first + block_rows
        scores = (
            jnp.einsum(
                "qhgd,khd->hgqk",
                query_heads[first:limit],
                key_heads[:limit],
                preferred_element_type=jnp.float32,
            )
            * factor
        )
        visible = jnp.arange(limit)[None, :] <= (first + jnp.arange(block_rows))[:, None]
        scores = jnp.where(visible, scores, -1e30)
        shifted = jnp.exp(scores - jnp.max(scores, axis=-1, keepdims=True))
        probs = shifted / jnp.sum(shifted, axis=-1, keepdims=True)
        rounded = probs.astype(jnp.bfloat16)
        context = jnp.einsum(
            "hgqk,khd->qhgd", rounded, value_heads[:limit], preferred_element_type=jnp.float32
        )
        pieces.append(context.reshape(block_rows, -1))
        kept.append(probs)
    return (jnp.concatenate(pieces, axis=0), kept)


def attend_back(incoming_all, queries, keys, values, kept, groups, factor):
    length = queries.shape[0]
    heads_kv = keys.shape[1] // HEAD
    query_heads = queries.reshape(length, heads_kv, groups, HEAD)
    key_heads = keys.reshape(length, heads_kv, HEAD)
    value_heads = values.reshape(length, heads_kv, HEAD)
    block_rows = min(512, length)
    grad_keys = jnp.zeros((length, heads_kv, HEAD), jnp.float32)
    grad_values = jnp.zeros((length, heads_kv, HEAD), jnp.float32)
    query_parts = []
    for number in range(length // block_rows):
        first = number * block_rows
        limit = first + block_rows
        probs = kept[number]
        rounded = probs.astype(jnp.bfloat16)
        incoming = incoming_all[first:limit].reshape(block_rows, heads_kv, groups, HEAD)
        grad_values = grad_values.at[:limit].add(
            jnp.einsum("hgqk,qhgd->khd", rounded, incoming, preferred_element_type=jnp.float32)
        )
        grad_probs = jnp.einsum(
            "qhgd,khd->hgqk", incoming, value_heads[:limit], preferred_element_type=jnp.float32
        )
        grad_scores = probs * (grad_probs - jnp.sum(grad_probs * probs, axis=-1, keepdims=True))
        scaled = (grad_scores * factor).astype(jnp.bfloat16)
        query_parts.append(
            jnp.einsum(
                "hgqk,khd->qhgd", scaled, key_heads[:limit], preferred_element_type=jnp.float32
            ).reshape(block_rows, -1)
        )
        grad_keys = grad_keys.at[:limit].add(
            jnp.einsum(
                "hgqk,qhgd->khd",
                scaled,
                query_heads[first:limit],
                preferred_element_type=jnp.float32,
            )
        )
    grad_queries = jnp.concatenate(query_parts, axis=0).astype(jnp.bfloat16)
    return (
        grad_queries,
        grad_keys.reshape(length, -1).astype(jnp.bfloat16),
        grad_values.reshape(length, -1).astype(jnp.bfloat16),
    )


MESH = pl.DeviceIdType.MESH
FACTOR = HEAD ** (-0.5)
NT = (((1,), (1,)), ((), ()))
TN = (((0,), (0,)), ((), ()))


def dot(a, b, dims=(((1,), (0,)), ((), ()))):
    return lax.dot_general(a, b, dims, preferred_element_type=jnp.float32)


def lanes(start, size=HEAD):
    return pl.ds(pl.multiple_of(start, HEAD), size)


def fused(
    dp_count,
    t_count,
    tq,
    tk,
    tv,
    proj,
    xin,
    win,
    out,
    wbuf,
    xall,
    ctx,
    ptile,
    stage,
    tgt,
    sib,
    from_left,
    from_right,
    acc,
    qkv,
    grads,
    gkv,
    loc_sem,
    tile_sem,
    x_send,
    x_recv,
    t_send,
    t_recv,
    wl_send,
    wl_recv,
    wr_send,
    wr_recv,
    ws_send,
    ws_recv,
    gs_send,
    gs_recv,
    gl_send,
    gl_recv,
    gr_send,
    gr_recv,
):
    line = dp_count // 2
    groups = win.shape[0]
    width = win.shape[2]
    rows = win.shape[1]
    length = tq.shape[0]
    share = xin.shape[0]
    ratio = width // HEAD - 2
    t_heads = tq.shape[1] // HEAD
    t_ratio = t_heads // (tk.shape[1] // HEAD)
    cols = stage.shape[2]
    tile = ptile.shape[2]
    dp = lax.axis_index("dp")
    ten = lax.axis_index("tensor")
    p = dp // 2
    c = dp % 2
    has_left = p > 0
    has_right = p < line - 1
    left = {"dp": dp - 2}
    right = {"dp": dp + 2}
    sibling = {"dp": dp + 1 - 2 * c}

    def peer(r):
        return {"tensor": lax.rem(ten + r, t_count)}

    def remote(src, dst, send, recv, device):
        return pltpu.make_async_remote_copy(
            src_ref=src,
            dst_ref=dst,
            send_sem=send,
            recv_sem=recv,
            device_id=device,
            device_id_type=MESH,
        )

    barrier = pltpu.get_barrier_semaphore()

    def hello(device):
        pl.semaphore_signal(barrier, inc=1, device_id=device, device_id_type=MESH)

    @pl.when(has_left)
    def _():
        hello(left)

    @pl.when(has_right)
    def _():
        hello(right)

    hello(sibling)
    for r in range(1, t_count):
        hello(peer(r))
    pl.semaphore_wait(
        barrier, t_count + has_left.astype(jnp.int32) + has_right.astype(jnp.int32)
    )

    def w_left(g, s):
        spot = wbuf.at[g, dp + 2 * s]
        return remote(
            win.at[g] if s == 0 else spot,
            spot,
            wl_send.at[g, s],
            wl_recv.at[g, s],
            left,
        )

    def w_right(g, s):
        spot = wbuf.at[g, dp - 2 * s]
        return remote(
            win.at[g] if s == 0 else spot,
            spot,
            wr_send.at[g, s],
            wr_recv.at[g, s],
            right,
        )

    def w_sib(g, o, own=False):
        spot = wbuf.at[g, 2 * o + c]
        return remote(
            win.at[g] if own else spot, spot, ws_send.at[g, o], ws_recv.at[g, o], sibling
        )

    def w_begin(g):
        @pl.when(has_left)
        def _():
            w_left(g, 0).start()

        @pl.when(has_right)
        def _():
            w_right(g, 0).start()

        w_sib(g, p, True).start()

    def w_step(g, s):
        @pl.when(p >= s)
        def _():
            spot = wbuf.at[g, dp - 2 * s]
            remote(spot, spot, wr_send.at[g, s], wr_recv.at[g, s - 1], right).wait_recv()

            @pl.when(has_right)
            def _():
                w_right(g, s).start()

            w_sib(g, p - s).start()

        @pl.when(p + s < line)
        def _():
            spot = wbuf.at[g, dp + 2 * s]
            remote(spot, spot, wl_send.at[g, s], wl_recv.at[g, s - 1], left).wait_recv()

            @pl.when(has_left)
            def _():
                w_left(g, s).start()

            w_sib(g, p + s).start()

    def w_finish(g):
        for s in range(line):

            @pl.when(has_left & (p + s < line))
            def _():
                w_left(g, s).wait_send()

            @pl.when(has_right & (p >= s))
            def _():
                w_right(g, s).wait_send()

        for o in range(line):
            w_sib(g, o).wait_send()
            spot = wbuf.at[g, 2 * o + 1 - c]
            remote(spot, spot, ws_send.at[g, o], ws_recv.at[g, o], sibling).wait_recv()
        pltpu.make_async_copy(win.at[g], wbuf.at[g, dp], loc_sem.at[g]).wait()

    def x_spot(t):
        return xall.at[pl.ds(pl.multiple_of(t * share, 16), share)]

    def x_copy(r):
        return remote(xin, x_spot(ten), x_send.at[r - 1], x_recv.at[r - 1], peer(r))

    def x_wait():
        for r in range(1, t_count):
            x_copy(r).wait_send()
            spot = x_spot(lax.rem(ten + t_count - r, t_count))
            remote(spot, spot, x_send.at[r - 1], x_recv.at[r - 1], peer(r)).wait_recv()
        pltpu.make_async_copy(xin, x_spot(ten), loc_sem.at[groups]).wait()

    def t_copy(r):
        return remote(stage.at[r], tgt.at[r - 1], t_send.at[r - 1], t_recv.at[r - 1], peer(r))

    w_begin(0)
    for r in range(1, t_count):
        x_copy(r).start()
    for g in range(groups):
        pltpu.make_async_copy(win.at[g], wbuf.at[g, dp], loc_sem.at[g]).start()
    pltpu.make_async_copy(xin, x_spot(ten), loc_sem.at[groups]).start()

    per_owner = cols // tile
    tiles = t_count * per_owner

    def tile_copy(i):
        owner = lax.rem(ten + 1 + i // per_owner, t_count)
        return pltpu.make_async_copy(
            proj.at[:, lanes(owner * cols + (i % per_owner) * tile, tile)],
            ptile.at[i % 2],
            tile_sem.at[i % 2],
        )

    tile_copy(0).start()
    tile_copy(1).start()

    visible = lax.broadcasted_iota(jnp.int32, (length, length), 1) <= lax.broadcasted_iota(
        jnp.int32, (length, length), 0
    )

    def weigh(q, k):
        scores = jnp.where(visible, dot(q, k, NT) * FACTOR, -1e30)
        shifted = jnp.exp(scores - jnp.max(scores, axis=-1, keepdims=True))
        return shifted, jnp.sum(shifted, axis=-1, keepdims=True)

    def teacher_head(h, carry):
        kv = lanes((h // t_ratio) * HEAD)
        shifted, total = weigh(tq[:, lanes(h * HEAD)], tk[:, kv])
        ctx[:, lanes(h * HEAD)] = (
            dot(shifted.astype(jnp.bfloat16), tv[:, kv]) / total
        ).astype(jnp.bfloat16)
        return carry

    lax.fori_loop(0, t_heads // 2, teacher_head, 0)
    w_step(0, 1)
    lax.fori_loop(t_heads // 2, t_heads, teacher_head, 0)
    for i in range(tiles):
        tile_copy(i).wait()
        r = (1 + i // per_owner) % t_count
        stage[r, :, pl.ds((i % per_owner) * tile, tile)] = dot(ctx[...], ptile[i % 2]).astype(
            jnp.bfloat16
        )
        if i + 2 < tiles:
            tile_copy(i + 2).start()
        if r and i % per_owner == per_owner - 1:
            t_copy(r).start()
        if i == tiles // 4:
            for s in range(2, line - 1):
                w_step(0, s)
            if groups > 1:
                w_begin(1)
    if line > 2:
        w_step(0, line - 1)
    x_wait()

    def x_cols(d):
        return xall[:, lanes(d * rows, rows)]

    def project(g):
        acc[...] = dot(x_cols(0), wbuf[g, 0])

        def one(d, carry):
            acc[...] += dot(x_cols(d), wbuf[g, d])
            return carry

        lax.fori_loop(1, dp_count, one, 0)
        qkv[...] = acc[...].astype(jnp.bfloat16)

    def heads(g, first, last):
        def one(j, carry):
            q = qkv[:, lanes(j * HEAD)]
            k = qkv[:, pl.ds(ratio * HEAD, HEAD)]
            v = qkv[:, pl.ds((ratio + 1) * HEAD, HEAD)]
            shifted, total = weigh(q, k)
            probs = shifted / total
            rounded = probs.astype(jnp.bfloat16)
            spot = lanes((g * ratio + j) * HEAD)
            target = stage[0, :, spot].astype(jnp.float32)
            for r in range(t_count - 1):
                target += tgt[r, :, spot].astype(jnp.float32)
            incoming = ((dot(rounded, v) - target) / dp_count).astype(jnp.bfloat16)
            gkv[1] += dot(rounded, incoming, TN)
            grad = dot(incoming, v, NT)
            grad = probs * (grad - jnp.sum(grad * probs, axis=-1, keepdims=True))
            scaled = (grad * FACTOR).astype(jnp.bfloat16)
            grads[:, lanes(j * HEAD)] = dot(scaled, k).astype(jnp.bfloat16)
            gkv[0] += dot(scaled, q, TN)
            return carry

        lax.fori_loop(first, last, one, 0)

    def g_sib(g, o):
        return remote(
            wbuf.at[g, 2 * o + 1 - c], sib.at[g, o], gs_send.at[g, o], gs_recv.at[g, o], sibling
        )

    def g_right(g, k):
        o = line - 1 - k
        slot = o - p - 1
        return remote(
            wbuf.at[g, 2 * o + c],
            from_left.at[g, slot],
            gr_send.at[g, k],
            gr_recv.at[g, slot],
            right,
        )

    def g_left(g, k):
        slot = p - 1 - k
        return remote(
            wbuf.at[g, 2 * k + c],
            from_right.at[g, slot],
            gl_send.at[g, k],
            gl_recv.at[g, slot],
            left,
        )

    def wait_left(g, slot):
        spot = from_left.at[g, slot]
        remote(spot, spot, gr_send.at[g, 0], gr_recv.at[g, slot], right).wait_recv()

    def wait_right(g, slot):
        spot = from_right.at[g, slot]
        remote(spot, spot, gl_send.at[g, 0], gl_recv.at[g, slot], left).wait_recv()

    def products(g):
        for j in range(2):
            grads[:, pl.ds((ratio + j) * HEAD, HEAD)] = gkv[j].astype(jnp.bfloat16)

        def one(i, carry):
            o = jnp.where(i % 2 == 0, i // 2, line - 1 - i // 2)
            d = 2 * o + 1 - c
            wbuf[g, d] = dot(x_cols(d), grads[...], TN).astype(jnp.bfloat16)
            g_sib(g, o).start()
            d = 2 * o + c
            wbuf[g, d] = dot(x_cols(d), grads[...], TN).astype(jnp.bfloat16)
            return carry

        lax.fori_loop(0, line, one, 0)

    def pair(g, o):
        g_sib(g, o).wait_recv()
        return wbuf[g, 2 * o + c].astype(jnp.float32) + sib[g, o].astype(jnp.float32)

    def g_step(g, k):
        o = line - 1 - k

        @pl.when(o > p)
        def _():
            wbuf[g, 2 * o + c] = pair(g, o).astype(jnp.bfloat16)

            @pl.when(has_left)
            def _():
                wait_left(g, o - p)
                wbuf[g, 2 * o + c] = (
                    wbuf[g, 2 * o + c].astype(jnp.float32)
                    + from_left[g, o - p].astype(jnp.float32)
                ).astype(jnp.bfloat16)

            g_right(g, k).start()

        @pl.when(k < p)
        def _():
            wbuf[g, 2 * k + c] = pair(g, k).astype(jnp.bfloat16)

            @pl.when(has_right)
            def _():
                wait_right(g, p - k)
                wbuf[g, 2 * k + c] = (
                    wbuf[g, 2 * k + c].astype(jnp.float32)
                    + from_right[g, p - k].astype(jnp.float32)
                ).astype(jnp.bfloat16)

            g_left(g, k).start()

    def g_finish(g):
        out[g] = pair(g, p)

        @pl.when(has_left)
        def _():
            wait_left(g, 0)
            out[g] += from_left[g, 0].astype(jnp.float32)

        @pl.when(has_right)
        def _():
            wait_right(g, 0)
            out[g] += from_right[g, 0].astype(jnp.float32)

        for k in range(line - 1):

            @pl.when(line - 1 - k > p)
            def _():
                g_right(g, k).wait_send()

            @pl.when(k < p)
            def _():
                g_left(g, k).wait_send()

        for o in range(line):
            g_sib(g, o).wait_send()

    for g in range(groups):
        work = []
        if g:
            work += [functools.partial(g_step, g - 1, k) for k in range(line - 1)]
            work += [functools.partial(g_finish, g - 1)]
        if g + 1 < groups:
            work += [functools.partial(w_step, g + 1, s) for s in range(1, line)]
        if g > 0 and g + 1 < groups:
            w_begin(g + 1)
        w_finish(g)
        if g and work:
            work.pop(0)()
        project(g)
        if g == 0:
            for r in range(1, t_count):
                t_copy(r).wait()
        gkv[...] = jnp.zeros_like(gkv)
        for j in range(ratio):
            if work:
                work.pop(0)()
            heads(g, j, j + 1)
        while work:
            work.pop(0)()
        products(g)
    for k in range(line - 1):
        g_step(groups - 1, k)
    g_finish(groups - 1)


def fused_call(tq, tk, tv, projector, xin, query_weight, key_weight, value_weight):
    dp_count = lax.axis_size("dp")
    t_count = lax.axis_size("tensor")
    line = dp_count // 2
    groups = key_weight.shape[1] // HEAD
    rows = query_weight.shape[0]
    q_cols = query_weight.shape[1]
    per = q_cols // groups
    width = per + 2 * HEAD
    length = tq.shape[0]
    win = jnp.concatenate(
        [
            query_weight.reshape(rows, groups, per),
            key_weight.reshape(rows, groups, HEAD),
            value_weight.reshape(rows, groups, HEAD),
        ],
        axis=2,
    ).transpose(1, 0, 2)
    cols = projector.shape[1] // t_count
    tile = min(512, cols)
    bf = jnp.bfloat16
    vmem = pl.BlockSpec(memory_space=pltpu.VMEM)
    hbm = pl.BlockSpec(memory_space=pl.ANY)
    sem = pltpu.SemaphoreType.DMA
    out = pl.pallas_call(
        functools.partial(fused, dp_count, t_count),
        out_shape=jax.ShapeDtypeStruct((groups, rows, width), jnp.float32),
        in_specs=[vmem, vmem, vmem, hbm, hbm, hbm],
        out_specs=vmem,
        scratch_shapes=[
            pltpu.VMEM((groups, dp_count, rows, width), bf),
            pltpu.VMEM((length, xin.shape[1]), bf),
            pltpu.VMEM(tq.shape, bf),
            pltpu.VMEM((2, projector.shape[0], tile), bf),
            pltpu.VMEM((t_count, length, cols), bf),
            pltpu.VMEM((t_count - 1, length, cols), bf),
            pltpu.VMEM((groups, line, rows, width), bf),
            pltpu.VMEM((groups, line - 1, rows, width), bf),
            pltpu.VMEM((groups, line - 1, rows, width), bf),
            pltpu.VMEM((length, width), jnp.float32),
            pltpu.VMEM((length, width), bf),
            pltpu.VMEM((length, width), bf),
            pltpu.VMEM((2, length, HEAD), jnp.float32),
            sem((groups + 1,)),
            sem((2,)),
            sem((t_count - 1,)),
            sem((t_count - 1,)),
            sem((t_count - 1,)),
            sem((t_count - 1,)),
        ]
        + [sem((groups, line))] * 12,
        compiler_params=pltpu.CompilerParams(
            collective_id=0, has_side_effects=True, vmem_limit_bytes=VMEM_LIMIT
        ),
    )(tq, tk, tv, projector, xin, win)
    return (
        jnp.concatenate([out[g, :, :per] for g in range(groups)], axis=1),
        jnp.concatenate([out[g, :, per : per + HEAD] for g in range(groups)], axis=1),
        jnp.concatenate([out[g, :, per + HEAD :] for g in range(groups)], axis=1),
    )


def per_device(
    teacher_queries,
    teacher_keys,
    teacher_values,
    projector,
    student_inputs,
    query_weight,
    key_weight,
    value_weight,
):
    if teacher_queries.shape[1] <= 512:
        return fused_call(
            teacher_queries[0],
            teacher_keys[0],
            teacher_values[0],
            projector,
            student_inputs[0],
            query_weight,
            key_weight,
            value_weight,
        )
    factor = HEAD ** (-0.5)
    dp_count = lax.axis_size("dp")
    context_t, unused = attend(
        teacher_queries[0], teacher_keys[0], teacher_values[0], TQH // TKVH, factor
    )
    context_t = context_t.astype(jnp.bfloat16)
    summed = lax.psum_scatter(
        lax.dot_general(
            projector, context_t, (((0,), (1,)), ((), ())), preferred_element_type=jnp.float32
        ).astype(jnp.bfloat16),
        "tensor",
        scatter_dimension=0,
        tiled=True,
    ).astype(jnp.float32)
    target = summed.T
    rows_all = lax.all_gather(student_inputs[0], "tensor", axis=0, tiled=True)
    full_weights = (
        lax.all_gather(query_weight, "dp", axis=0, tiled=True),
        lax.all_gather(key_weight, "dp", axis=0, tiled=True),
        lax.all_gather(value_weight, "dp", axis=0, tiled=True),
    )
    rows_all, full_weights = (rows_all, full_weights)
    queries = jnp.dot(rows_all, full_weights[0], preferred_element_type=jnp.float32).astype(
        jnp.bfloat16
    )
    keys = jnp.dot(rows_all, full_weights[1], preferred_element_type=jnp.float32).astype(
        jnp.bfloat16
    )
    values = jnp.dot(rows_all, full_weights[2], preferred_element_type=jnp.float32).astype(
        jnp.bfloat16
    )
    context_s, kept = attend(queries, keys, values, SQH // SKVH, factor)
    grad_context = ((context_s - target) / dp_count).astype(jnp.bfloat16)
    grad_q, grad_k, grad_v = attend_back(
        grad_context, queries, keys, values, kept, SQH // SKVH, factor
    )
    grad_all = jnp.concatenate([grad_q, grad_k, grad_v], axis=1)
    whole = lax.dot_general(
        rows_all, grad_all, (((0,), (0,)), ((), ())), preferred_element_type=jnp.float32
    )
    reduced = lax.psum_scatter(
        whole.astype(jnp.bfloat16), "dp", scatter_dimension=0, tiled=True
    ).astype(jnp.float32)
    query_cols = query_weight.shape[1]
    key_cols = key_weight.shape[1]
    return (
        reduced[:, :query_cols],
        reduced[:, query_cols : query_cols + key_cols],
        reduced[:, query_cols + key_cols :],
    )


def solution(mesh):
    placed = (
        P("dp", None, "tensor"),
        P("dp", None, "tensor"),
        P("dp", None, "tensor"),
        P("tensor", None),
        P("dp", "tensor", None),
        P("dp", "tensor"),
        P("dp", "tensor"),
        P("dp", "tensor"),
    )
    return jax.shard_map(
        per_device,
        mesh=mesh,
        in_specs=placed,
        out_specs=(P("dp", "tensor"), P("dp", "tensor"), P("dp", "tensor")),
        check_vma=False,
    )
```

```python
import functools

import jax
import jax.numpy as jnp
from jax import lax
from jax.experimental import pallas as pl
from jax.experimental.pallas import tpu as pltpu
from jax.sharding import PartitionSpec as P

HEAD = 128
TQH = 64
TKVH = 8
SQH = 32
SKVH = 8
VMEM_LIMIT = 63 * 1024 * 1024


def attend(queries, keys, values, groups, factor):
    length = queries.shape[0]
    heads_kv = keys.shape[1] // HEAD
    query_heads = queries.reshape(length, heads_kv, groups, HEAD)
    key_heads = keys.reshape(length, heads_kv, HEAD)
    value_heads = values.reshape(length, heads_kv, HEAD)
    block_rows = min(512, length)
    pieces = []
    kept = []
    for number in range(length // block_rows):
        first = number * block_rows
        limit = first + block_rows
        scores = (
            jnp.einsum(
                "qhgd,khd->hgqk",
                query_heads[first:limit],
                key_heads[:limit],
                preferred_element_type=jnp.float32,
            )
            * factor
        )
        visible = jnp.arange(limit)[None, :] <= (first + jnp.arange(block_rows))[:, None]
        scores = jnp.where(visible, scores, -1e30)
        shifted = jnp.exp(scores - jnp.max(scores, axis=-1, keepdims=True))
        probs = shifted / jnp.sum(shifted, axis=-1, keepdims=True)
        rounded = probs.astype(jnp.bfloat16)
        context = jnp.einsum(
            "hgqk,khd->qhgd", rounded, value_heads[:limit], preferred_element_type=jnp.float32
        )
        pieces.append(context.reshape(block_rows, -1))
        kept.append(probs)
    return (jnp.concatenate(pieces, axis=0), kept)


def attend_back(incoming_all, queries, keys, values, kept, groups, factor):
    length = queries.shape[0]
    heads_kv = keys.shape[1] // HEAD
    query_heads = queries.reshape(length, heads_kv, groups, HEAD)
    key_heads = keys.reshape(length, heads_kv, HEAD)
    value_heads = values.reshape(length, heads_kv, HEAD)
    block_rows = min(512, length)
    grad_keys = jnp.zeros((length, heads_kv, HEAD), jnp.float32)
    grad_values = jnp.zeros((length, heads_kv, HEAD), jnp.float32)
    query_parts = []
    for number in range(length // block_rows):
        first = number * block_rows
        limit = first + block_rows
        probs = kept[number]
        rounded = probs.astype(jnp.bfloat16)
        incoming = incoming_all[first:limit].reshape(block_rows, heads_kv, groups, HEAD)
        grad_values = grad_values.at[:limit].add(
            jnp.einsum("hgqk,qhgd->khd", rounded, incoming, preferred_element_type=jnp.float32)
        )
        grad_probs = jnp.einsum(
            "qhgd,khd->hgqk", incoming, value_heads[:limit], preferred_element_type=jnp.float32
        )
        grad_scores = probs * (grad_probs - jnp.sum(grad_probs * probs, axis=-1, keepdims=True))
        scaled = (grad_scores * factor).astype(jnp.bfloat16)
        query_parts.append(
            jnp.einsum(
                "hgqk,khd->qhgd", scaled, key_heads[:limit], preferred_element_type=jnp.float32
            ).reshape(block_rows, -1)
        )
        grad_keys = grad_keys.at[:limit].add(
            jnp.einsum(
                "hgqk,qhgd->khd",
                scaled,
                query_heads[first:limit],
                preferred_element_type=jnp.float32,
            )
        )
    grad_queries = jnp.concatenate(query_parts, axis=0).astype(jnp.bfloat16)
    return (
        grad_queries,
        grad_keys.reshape(length, -1).astype(jnp.bfloat16),
        grad_values.reshape(length, -1).astype(jnp.bfloat16),
    )


MESH = pl.DeviceIdType.MESH
FACTOR = HEAD ** (-0.5)
NT = (((1,), (1,)), ((), ()))
TN = (((0,), (0,)), ((), ()))


def dot(a, b, dims=(((1,), (0,)), ((), ()))):
    return lax.dot_general(a, b, dims, preferred_element_type=jnp.float32)


def lanes(start, size=HEAD):
    return pl.ds(pl.multiple_of(start, HEAD), size)


def fused(
    dp_count,
    t_count,
    tq,
    tk,
    tv,
    proj,
    xin,
    win,
    out,
    wbuf,
    xall,
    ctx,
    ptile,
    stage,
    tgt,
    sib,
    from_left,
    from_right,
    acc,
    qkv,
    grads,
    gkv,
    loc_sem,
    tile_sem,
    x_send,
    x_recv,
    t_send,
    t_recv,
    wl_send,
    wl_recv,
    wr_send,
    wr_recv,
    ws_send,
    ws_recv,
    gs_send,
    gs_recv,
    gl_send,
    gl_recv,
    gr_send,
    gr_recv,
):
    line = dp_count // 2
    groups = win.shape[0]
    width = win.shape[2]
    rows = win.shape[1]
    length = tq.shape[0]
    share = xin.shape[0]
    ratio = width // HEAD - 2
    t_heads = tq.shape[1] // HEAD
    t_ratio = t_heads // (tk.shape[1] // HEAD)
    cols = stage.shape[2]
    tile = ratio * HEAD
    dp = lax.axis_index("dp")
    ten = lax.axis_index("tensor")
    p = dp // 2
    c = dp % 2
    has_left = p > 0
    has_right = p < line - 1
    left = {"dp": dp - 2}
    right = {"dp": dp + 2}
    sibling = {"dp": dp + 1 - 2 * c}

    def peer(r):
        return {"tensor": lax.rem(ten + r, t_count)}

    def remote(src, dst, send, recv, device):
        return pltpu.make_async_remote_copy(
            src_ref=src,
            dst_ref=dst,
            send_sem=send,
            recv_sem=recv,
            device_id=device,
            device_id_type=MESH,
        )

    barrier = pltpu.get_barrier_semaphore()

    def hello(device):
        pl.semaphore_signal(barrier, inc=1, device_id=device, device_id_type=MESH)

    @pl.when(has_left)
    def _():
        hello(left)

    @pl.when(has_right)
    def _():
        hello(right)

    hello(sibling)
    for r in range(1, t_count):
        hello(peer(r))
    pl.semaphore_wait(
        barrier, t_count + has_left.astype(jnp.int32) + has_right.astype(jnp.int32)
    )

    def w_left(g, s):
        spot = wbuf.at[g, dp + 2 * s]
        return remote(
            win.at[g] if s == 0 else spot,
            spot,
            wl_send.at[g, s],
            wl_recv.at[g, s],
            left,
        )

    def w_right(g, s):
        spot = wbuf.at[g, dp - 2 * s]
        return remote(
            win.at[g] if s == 0 else spot,
            spot,
            wr_send.at[g, s],
            wr_recv.at[g, s],
            right,
        )

    def w_sib(g, o, own=False):
        spot = wbuf.at[g, 2 * o + c]
        return remote(
            win.at[g] if own else spot, spot, ws_send.at[g, o], ws_recv.at[g, o], sibling
        )

    def w_begin(g):
        @pl.when(has_left)
        def _():
            w_left(g, 0).start()

        @pl.when(has_right)
        def _():
            w_right(g, 0).start()

        w_sib(g, p, True).start()

    def w_step(g, s):
        @pl.when(p >= s)
        def _():
            spot = wbuf.at[g, dp - 2 * s]
            remote(spot, spot, wr_send.at[g, s], wr_recv.at[g, s - 1], right).wait_recv()

            @pl.when(has_right)
            def _():
                w_right(g, s).start()

            w_sib(g, p - s).start()

        @pl.when(p + s < line)
        def _():
            spot = wbuf.at[g, dp + 2 * s]
            remote(spot, spot, wl_send.at[g, s], wl_recv.at[g, s - 1], left).wait_recv()

            @pl.when(has_left)
            def _():
                w_left(g, s).start()

            w_sib(g, p + s).start()

    def w_finish(g):
        for s in range(line):

            @pl.when(has_left & (p + s < line))
            def _():
                w_left(g, s).wait_send()

            @pl.when(has_right & (p >= s))
            def _():
                w_right(g, s).wait_send()

        for o in range(line):
            w_sib(g, o).wait_send()
            spot = wbuf.at[g, 2 * o + 1 - c]
            remote(spot, spot, ws_send.at[g, o], ws_recv.at[g, o], sibling).wait_recv()
        pltpu.make_async_copy(win.at[g], wbuf.at[g, dp], loc_sem.at[g]).wait()

    def x_spot(t):
        return xall.at[pl.ds(pl.multiple_of(t * share, 16), share)]

    def x_copy(r):
        return remote(xin, x_spot(ten), x_send.at[r - 1], x_recv.at[r - 1], peer(r))

    def x_wait():
        for r in range(1, t_count):
            x_copy(r).wait_send()
            spot = x_spot(lax.rem(ten + t_count - r, t_count))
            remote(spot, spot, x_send.at[r - 1], x_recv.at[r - 1], peer(r)).wait_recv()
        pltpu.make_async_copy(xin, x_spot(ten), loc_sem.at[groups]).wait()

    def t_copy(r, part):
        spot = pl.ds(part * tile, tile)
        return remote(
            stage.at[r, :, spot],
            tgt.at[r - 1, :, spot],
            t_send.at[r - 1, part],
            t_recv.at[r - 1, part],
            peer(r),
        )

    w_begin(0)
    for r in range(1, t_count):
        x_copy(r).start()
    for g in range(groups):
        pltpu.make_async_copy(win.at[g], wbuf.at[g, dp], loc_sem.at[g]).start()
    pltpu.make_async_copy(xin, x_spot(ten), loc_sem.at[groups]).start()

    tiles = t_count * (cols // tile)
    deep = proj.shape[0]

    def tile_spot(i):
        return pl.ds((i % 2) * deep, deep), pl.ds(0, tile)

    def tile_copy(i):
        owner = lax.rem(ten + 1 + i % t_count, t_count)
        return pltpu.make_async_copy(
            proj.at[:, lanes(owner * cols + (i // t_count) * tile, tile)],
            ptile.at[tile_spot(i)],
            tile_sem.at[i % 2],
        )

    tile_copy(0).start()
    tile_copy(1).start()

    def weigh(q, k, first):
        shape = (q.shape[0], k.shape[0])
        visible = lax.broadcasted_iota(jnp.int32, shape, 1) <= first + lax.broadcasted_iota(
            jnp.int32, shape, 0
        )
        scores = jnp.where(visible, dot(q, k, NT) * FACTOR, -1e30)
        shifted = jnp.exp(scores - jnp.max(scores, axis=-1, keepdims=True))
        return shifted, 1.0 / jnp.sum(shifted, axis=-1, keepdims=True)

    half = length // 2 if length % 512 == 0 else length
    blocks = [(first, first + half) for first in range(0, length, half)]

    def teacher_head(h, carry):
        kv = lanes((h // t_ratio) * HEAD)
        spot = lanes(h * HEAD)
        for first, limit in blocks:
            shifted, inverse = weigh(tq[first:limit, spot], tk[:limit, kv], first)
            ctx[first:limit, spot] = (
                dot(shifted.astype(jnp.bfloat16), tv[:limit, kv]) * inverse
            ).astype(jnp.bfloat16)
        return carry

    lax.fori_loop(0, 3 * t_heads // 4, teacher_head, 0)
    w_step(0, 1)
    lax.fori_loop(3 * t_heads // 4, t_heads, teacher_head, 0)
    for i in range(tiles):
        tile_copy(i).wait()
        r = (1 + i) % t_count
        part = i // t_count
        stage[r, :, pl.ds(part * tile, tile)] = dot(ctx[...], ptile[tile_spot(i)]).astype(
            jnp.bfloat16
        )
        if i + 2 < tiles:
            tile_copy(i + 2).start()
        if r:
            t_copy(r, part).start()
    for s in range(2, line - 1):
        w_step(0, s)
    if groups > 1:
        w_begin(1)
    x_wait()

    def x_turned(d):
        return ptile[pl.ds(pl.multiple_of(d * rows, rows), rows), pl.ds(0, length)]

    def turn(d, carry):
        ptile[pl.ds(pl.multiple_of(d * rows, rows), rows), pl.ds(0, length)] = x_cols(d).T
        return carry

    def x_cols(d):
        return xall[:, lanes(d * rows, rows)]

    lax.fori_loop(0, dp_count, turn, 0)
    if line > 2:
        w_step(0, line - 1)

    def project(g):
        acc[...] = dot(x_cols(0), wbuf[g, 0])

        def one(d, carry):
            acc[...] += dot(x_cols(d), wbuf[g, d])
            return carry

        lax.fori_loop(1, dp_count, one, 0)
        qkv[...] = acc[...].astype(jnp.bfloat16)

    def heads(g, begin, end):
        def one(j, carry):
            lane = lanes(j * HEAD)
            spot = lanes((g * ratio + j) * HEAD)
            for first, limit in blocks:
                q = qkv[first:limit, lane]
                k = qkv[:limit, pl.ds(ratio * HEAD, HEAD)]
                v = qkv[:limit, pl.ds((ratio + 1) * HEAD, HEAD)]
                shifted, inverse = weigh(q, k, first)
                probs = shifted * inverse
                rounded = probs.astype(jnp.bfloat16)
                target = stage[0, first:limit, spot].astype(jnp.float32)
                for r in range(t_count - 1):
                    target += tgt[r, first:limit, spot].astype(jnp.float32)
                incoming = ((dot(rounded, v) - target) / dp_count).astype(jnp.bfloat16)
                gkv[1, :limit] += dot(rounded, incoming, TN)
                grad = dot(incoming, v, NT)
                grad = probs * (grad - jnp.sum(grad * probs, axis=-1, keepdims=True))
                scaled = (grad * FACTOR).astype(jnp.bfloat16)
                grads[first:limit, lane] = dot(scaled, k).astype(jnp.bfloat16)
                gkv[0, :limit] += dot(scaled, q, TN)
            return carry

        lax.fori_loop(begin, end, one, 0)

    early = ratio - 1

    def cut(ref, q, i):
        spot = pl.ds(0, early * HEAD) if q % 2 == 0 else pl.ds(early * HEAD, 3 * HEAD)
        return ref.at[q // 2, i, :, spot]

    def g_sib(q, o):
        return remote(
            cut(wbuf, q, 2 * o + 1 - c),
            cut(sib, q, o),
            gs_send.at[q, o],
            gs_recv.at[q, o],
            sibling,
        )

    def g_right(q, k):
        o = line - 1 - k
        slot = o - p - 1
        return remote(
            cut(wbuf, q, 2 * o + c),
            cut(from_left, q, slot),
            gr_send.at[q, k],
            gr_recv.at[q, slot],
            right,
        )

    def g_left(q, k):
        slot = p - 1 - k
        return remote(
            cut(wbuf, q, 2 * k + c),
            cut(from_right, q, slot),
            gl_send.at[q, k],
            gl_recv.at[q, slot],
            left,
        )

    def wait_left(q, slot):
        spot = cut(from_left, q, slot)
        remote(spot, spot, gr_send.at[q, 0], gr_recv.at[q, slot], right).wait_recv()
        return spot[...].astype(jnp.float32)

    def wait_right(q, slot):
        spot = cut(from_right, q, slot)
        remote(spot, spot, gl_send.at[q, 0], gl_recv.at[q, slot], left).wait_recv()
        return spot[...].astype(jnp.float32)

    def pair(q, o):
        g_sib(q, o).wait_recv()
        return cut(wbuf, q, 2 * o + c)[...].astype(jnp.float32) + cut(sib, q, o)[...].astype(
            jnp.float32
        )

    def products(q):
        if q % 2:
            for j in range(2):
                grads[:, pl.ds((ratio + j) * HEAD, HEAD)] = gkv[j].astype(jnp.bfloat16)
            spot = pl.ds(early * HEAD, 3 * HEAD)
        else:
            spot = pl.ds(0, early * HEAD)

        def one(i, carry):
            o = jnp.where(i % 2 == 0, line - 1 - i // 2, i // 2)
            for core in (1 - c, c):
                d = 2 * o + core
                wbuf[q // 2, d, :, spot] = dot(x_turned(d), grads[:, spot]).astype(jnp.bfloat16)
                if core is not c:
                    g_sib(q, o).start()
            return carry

        lax.fori_loop(0, line, one, 0)

        @pl.when(p == 0)
        def _():
            for k in range(line - 1):
                spot = cut(wbuf, q, 2 * (line - 1 - k) + c)
                spot[...] = pair(q, line - 1 - k).astype(jnp.bfloat16)
                g_right(q, k).start()

        @pl.when(p == line - 1)
        def _():
            for k in range(line - 1):
                spot = cut(wbuf, q, 2 * k + c)
                spot[...] = pair(q, k).astype(jnp.bfloat16)
                g_left(q, k).start()

    def chain(q, k):
        o = line - 1 - k

        @pl.when(has_left & (o > p))
        def _():
            own = pair(q, o)
            spot = cut(wbuf, q, 2 * o + c)
            spot[...] = (own + wait_left(q, o - p)).astype(jnp.bfloat16)
            g_right(q, k).start()

        @pl.when(has_right & (k < p))
        def _():
            own = pair(q, k)
            spot = cut(wbuf, q, 2 * k + c)
            spot[...] = (own + wait_right(q, p - k)).astype(jnp.bfloat16)
            g_left(q, k).start()

    def finish(q):
        spot = pl.ds(0, early * HEAD) if q % 2 == 0 else pl.ds(early * HEAD, 3 * HEAD)
        total = out.at[q // 2, :, spot]
        total[...] = pair(q, p)

        @pl.when(has_left)
        def _():
            total[...] += wait_left(q, 0)

        @pl.when(has_right)
        def _():
            total[...] += wait_right(q, 0)

        for k in range(line - 1):

            @pl.when(line - 1 - k > p)
            def _():
                g_right(q, k).wait_send()

            @pl.when(k < p)
            def _():
                g_left(q, k).wait_send()

        for o in range(line):
            g_sib(q, o).wait_send()

    links = range(line - 2)
    for g in range(groups):
        work = []
        if g:
            for q in (2 * g - 2, 2 * g - 1):
                work += [functools.partial(chain, q, k) for k in links]
            work += [functools.partial(finish, 2 * g - 2), functools.partial(finish, 2 * g - 1)]
        ahead = []
        if g + 1 < groups:
            ahead = [functools.partial(w_step, g + 1, s) for s in range(1, line)]
            if g > 0:
                w_begin(g + 1)
        w_finish(g)
        if work:
            work.pop(0)()
        project(g)
        gkv[...] = jnp.zeros_like(gkv)
        for part in range(cols // tile):
            if (part * tile) // (ratio * HEAD) == g:
                for r in range(1, t_count):
                    t_copy(r, part).wait()
        for j in range(ratio):
            if work:
                work.pop(0)()
            if ahead and j % 2 == 0 and len(ahead) > 1:
                ahead.pop(0)()
            heads(g, j, j + 1)
            if j == early - 1:
                products(2 * g)
        products(2 * g + 1)
        while work:
            work.pop(0)()
        while ahead:
            ahead.pop(0)()
    for q in (2 * groups - 2, 2 * groups - 1):
        for k in links:
            chain(q, k)
    for q in (2 * groups - 2, 2 * groups - 1):
        finish(q)


def fused_call(tq, tk, tv, projector, xin, query_weight, key_weight, value_weight):
    dp_count = lax.axis_size("dp")
    t_count = lax.axis_size("tensor")
    line = dp_count // 2
    groups = key_weight.shape[1] // HEAD
    rows = query_weight.shape[0]
    q_cols = query_weight.shape[1]
    per = q_cols // groups
    width = per + 2 * HEAD
    length = tq.shape[0]
    win = jnp.concatenate(
        [
            query_weight.reshape(rows, groups, per),
            key_weight.reshape(rows, groups, HEAD),
            value_weight.reshape(rows, groups, HEAD),
        ],
        axis=2,
    ).transpose(1, 0, 2)
    cols = projector.shape[1] // t_count
    tile = min(per, cols)
    bf = jnp.bfloat16
    vmem = pl.BlockSpec(memory_space=pltpu.VMEM)
    hbm = pl.BlockSpec(memory_space=pl.ANY)
    sem = pltpu.SemaphoreType.DMA
    out = pl.pallas_call(
        functools.partial(fused, dp_count, t_count),
        out_shape=jax.ShapeDtypeStruct((groups, rows, width), jnp.float32),
        in_specs=[vmem, vmem, vmem, hbm, hbm, hbm],
        out_specs=vmem,
        scratch_shapes=[
            pltpu.VMEM((groups, dp_count, rows, width), bf),
            pltpu.VMEM((length, xin.shape[1]), bf),
            pltpu.VMEM(tq.shape, bf),
            pltpu.VMEM((max(2 * projector.shape[0], xin.shape[1]), max(tile, length)), bf),
            pltpu.VMEM((t_count, length, cols), bf),
            pltpu.VMEM((t_count - 1, length, cols), bf),
            pltpu.VMEM((groups, line, rows, width), bf),
            pltpu.VMEM((groups, line - 1, rows, width), bf),
            pltpu.VMEM((groups, line - 1, rows, width), bf),
            pltpu.VMEM((length, width), jnp.float32),
            pltpu.VMEM((length, width), bf),
            pltpu.VMEM((length, width), bf),
            pltpu.VMEM((2, length, HEAD), jnp.float32),
            sem((groups + 1,)),
            sem((2,)),
            sem((t_count - 1,)),
            sem((t_count - 1,)),
            sem((t_count - 1, cols // tile)),
            sem((t_count - 1, cols // tile)),
        ]
        + [sem((groups, line))] * 6
        + [sem((2 * groups, line))] * 6,
        compiler_params=pltpu.CompilerParams(
            collective_id=0, has_side_effects=True, vmem_limit_bytes=VMEM_LIMIT
        ),
    )(tq, tk, tv, projector, xin, win)
    return (
        jnp.concatenate([out[g, :, :per] for g in range(groups)], axis=1),
        jnp.concatenate([out[g, :, per : per + HEAD] for g in range(groups)], axis=1),
        jnp.concatenate([out[g, :, per + HEAD :] for g in range(groups)], axis=1),
    )


def per_device(
    teacher_queries,
    teacher_keys,
    teacher_values,
    projector,
    student_inputs,
    query_weight,
    key_weight,
    value_weight,
):
    if teacher_queries.shape[1] <= 512:
        return fused_call(
            teacher_queries[0],
            teacher_keys[0],
            teacher_values[0],
            projector,
            student_inputs[0],
            query_weight,
            key_weight,
            value_weight,
        )
    factor = HEAD ** (-0.5)
    dp_count = lax.axis_size("dp")
    context_t, unused = attend(
        teacher_queries[0], teacher_keys[0], teacher_values[0], TQH // TKVH, factor
    )
    context_t = context_t.astype(jnp.bfloat16)
    summed = lax.psum_scatter(
        lax.dot_general(
            projector, context_t, (((0,), (1,)), ((), ())), preferred_element_type=jnp.float32
        ).astype(jnp.bfloat16),
        "tensor",
        scatter_dimension=0,
        tiled=True,
    ).astype(jnp.float32)
    target = summed.T
    rows_all = lax.all_gather(student_inputs[0], "tensor", axis=0, tiled=True)
    full_weights = (
        lax.all_gather(query_weight, "dp", axis=0, tiled=True),
        lax.all_gather(key_weight, "dp", axis=0, tiled=True),
        lax.all_gather(value_weight, "dp", axis=0, tiled=True),
    )
    rows_all, full_weights = (rows_all, full_weights)
    queries = jnp.dot(rows_all, full_weights[0], preferred_element_type=jnp.float32).astype(
        jnp.bfloat16
    )
    keys = jnp.dot(rows_all, full_weights[1], preferred_element_type=jnp.float32).astype(
        jnp.bfloat16
    )
    values = jnp.dot(rows_all, full_weights[2], preferred_element_type=jnp.float32).astype(
        jnp.bfloat16
    )
    context_s, kept = attend(queries, keys, values, SQH // SKVH, factor)
    grad_context = ((context_s - target) / dp_count).astype(jnp.bfloat16)
    grad_q, grad_k, grad_v = attend_back(
        grad_context, queries, keys, values, kept, SQH // SKVH, factor
    )
    grad_all = jnp.concatenate([grad_q, grad_k, grad_v], axis=1)
    whole = lax.dot_general(
        rows_all, grad_all, (((0,), (0,)), ((), ())), preferred_element_type=jnp.float32
    )
    reduced = lax.psum_scatter(
        whole.astype(jnp.bfloat16), "dp", scatter_dimension=0, tiled=True
    ).astype(jnp.float32)
    query_cols = query_weight.shape[1]
    key_cols = key_weight.shape[1]
    return (
        reduced[:, :query_cols],
        reduced[:, query_cols : query_cols + key_cols],
        reduced[:, query_cols + key_cols :],
    )


def solution(mesh):
    placed = (
        P("dp", None, "tensor"),
        P("dp", None, "tensor"),
        P("dp", None, "tensor"),
        P("tensor", None),
        P("dp", "tensor", None),
        P("dp", "tensor"),
        P("dp", "tensor"),
        P("dp", "tensor"),
    )
    return jax.shard_map(
        per_device,
        mesh=mesh,
        in_specs=placed,
        out_specs=(P("dp", "tensor"), P("dp", "tensor"), P("dp", "tensor")),
        check_vma=False,
    )
```

```python
import functools

import jax
import jax.numpy as jnp
from jax import lax
from jax.experimental import pallas as pl
from jax.experimental.pallas import tpu as pltpu
from jax.sharding import PartitionSpec as P

HEAD = 128
TQH = 64
TKVH = 8
SQH = 32
SKVH = 8
VMEM_LIMIT = 63 * 1024 * 1024


def attend(queries, keys, values, groups, factor):
    length = queries.shape[0]
    heads_kv = keys.shape[1] // HEAD
    query_heads = queries.reshape(length, heads_kv, groups, HEAD)
    key_heads = keys.reshape(length, heads_kv, HEAD)
    value_heads = values.reshape(length, heads_kv, HEAD)
    block_rows = min(512, length)
    pieces = []
    kept = []
    for number in range(length // block_rows):
        first = number * block_rows
        limit = first + block_rows
        scores = (
            jnp.einsum(
                "qhgd,khd->hgqk",
                query_heads[first:limit],
                key_heads[:limit],
                preferred_element_type=jnp.float32,
            )
            * factor
        )
        visible = jnp.arange(limit)[None, :] <= (first + jnp.arange(block_rows))[:, None]
        scores = jnp.where(visible, scores, -1e30)
        shifted = jnp.exp(scores - jnp.max(scores, axis=-1, keepdims=True))
        probs = shifted / jnp.sum(shifted, axis=-1, keepdims=True)
        rounded = probs.astype(jnp.bfloat16)
        context = jnp.einsum(
            "hgqk,khd->qhgd", rounded, value_heads[:limit], preferred_element_type=jnp.float32
        )
        pieces.append(context.reshape(block_rows, -1))
        kept.append(probs)
    return (jnp.concatenate(pieces, axis=0), kept)


def attend_back(incoming_all, queries, keys, values, kept, groups, factor):
    length = queries.shape[0]
    heads_kv = keys.shape[1] // HEAD
    query_heads = queries.reshape(length, heads_kv, groups, HEAD)
    key_heads = keys.reshape(length, heads_kv, HEAD)
    value_heads = values.reshape(length, heads_kv, HEAD)
    block_rows = min(512, length)
    grad_keys = jnp.zeros((length, heads_kv, HEAD), jnp.float32)
    grad_values = jnp.zeros((length, heads_kv, HEAD), jnp.float32)
    query_parts = []
    for number in range(length // block_rows):
        first = number * block_rows
        limit = first + block_rows
        probs = kept[number]
        rounded = probs.astype(jnp.bfloat16)
        incoming = incoming_all[first:limit].reshape(block_rows, heads_kv, groups, HEAD)
        grad_values = grad_values.at[:limit].add(
            jnp.einsum("hgqk,qhgd->khd", rounded, incoming, preferred_element_type=jnp.float32)
        )
        grad_probs = jnp.einsum(
            "qhgd,khd->hgqk", incoming, value_heads[:limit], preferred_element_type=jnp.float32
        )
        grad_scores = probs * (grad_probs - jnp.sum(grad_probs * probs, axis=-1, keepdims=True))
        scaled = (grad_scores * factor).astype(jnp.bfloat16)
        query_parts.append(
            jnp.einsum(
                "hgqk,khd->qhgd", scaled, key_heads[:limit], preferred_element_type=jnp.float32
            ).reshape(block_rows, -1)
        )
        grad_keys = grad_keys.at[:limit].add(
            jnp.einsum(
                "hgqk,qhgd->khd",
                scaled,
                query_heads[first:limit],
                preferred_element_type=jnp.float32,
            )
        )
    grad_queries = jnp.concatenate(query_parts, axis=0).astype(jnp.bfloat16)
    return (
        grad_queries,
        grad_keys.reshape(length, -1).astype(jnp.bfloat16),
        grad_values.reshape(length, -1).astype(jnp.bfloat16),
    )


MESH = pl.DeviceIdType.MESH
FACTOR = HEAD ** (-0.5)
NT = (((1,), (1,)), ((), ()))
TN = (((0,), (0,)), ((), ()))


def dot(a, b, dims=(((1,), (0,)), ((), ()))):
    return lax.dot_general(a, b, dims, preferred_element_type=jnp.float32)


def lanes(start, size=HEAD):
    return pl.ds(pl.multiple_of(start, HEAD), size)


def fused(
    dp_count,
    t_count,
    tq,
    tk,
    tv,
    proj,
    xin,
    qw,
    kw,
    vw,
    out,
    wbuf,
    xall,
    ctx,
    ptile,
    stage,
    tgt,
    sib,
    from_left,
    from_right,
    acc,
    qkv,
    grads,
    gkv,
    loc_sem,
    tile_sem,
    x_send,
    x_recv,
    t_send,
    t_recv,
    wl_send,
    wl_recv,
    wr_send,
    wr_recv,
    ws_send,
    ws_recv,
    gs_send,
    gs_recv,
    gl_send,
    gl_recv,
    gr_send,
    gr_recv,
):
    line = dp_count // 2
    groups = wbuf.shape[0]
    width = wbuf.shape[3]
    rows = wbuf.shape[2]
    length = tq.shape[0]
    share = xin.shape[0]
    ratio = width // HEAD - 2
    t_heads = tq.shape[1] // HEAD
    t_ratio = t_heads // (tk.shape[1] // HEAD)
    cols = stage.shape[2]
    tile = ratio * HEAD
    dp = lax.axis_index("dp")
    ten = lax.axis_index("tensor")
    p = dp // 2
    c = dp % 2
    has_left = p > 0
    has_right = p < line - 1
    left = {"dp": dp - 2}
    right = {"dp": dp + 2}
    sibling = {"dp": dp + 1 - 2 * c}

    def peer(r):
        return {"tensor": lax.rem(ten + r, t_count)}

    def remote(src, dst, send, recv, device):
        return pltpu.make_async_remote_copy(
            src_ref=src,
            dst_ref=dst,
            send_sem=send,
            recv_sem=recv,
            device_id=device,
            device_id_type=MESH,
        )

    def own_copies(g):
        per = ratio * HEAD
        mine = wbuf.at[g, dp]
        return (
            pltpu.make_async_copy(
                qw.at[:, pl.ds(g * per, per)], mine.at[:, pl.ds(0, per)], loc_sem.at[g, 0]
            ),
            pltpu.make_async_copy(
                kw.at[:, pl.ds(g * HEAD, HEAD)], mine.at[:, pl.ds(per, HEAD)], loc_sem.at[g, 1]
            ),
            pltpu.make_async_copy(
                vw.at[:, pl.ds(g * HEAD, HEAD)],
                mine.at[:, pl.ds(per + HEAD, HEAD)],
                loc_sem.at[g, 2],
            ),
        )

    for g in range(groups):
        for copy in own_copies(g):
            copy.start()

    barrier = pltpu.get_barrier_semaphore()

    def hello(device):
        pl.semaphore_signal(barrier, inc=1, device_id=device, device_id_type=MESH)

    @pl.when(has_left)
    def _():
        hello(left)

    @pl.when(has_right)
    def _():
        hello(right)

    hello(sibling)
    for r in range(1, t_count):
        hello(peer(r))
    pl.semaphore_wait(
        barrier, t_count + has_left.astype(jnp.int32) + has_right.astype(jnp.int32)
    )

    def w_left(g, s):
        spot = wbuf.at[g, dp + 2 * s]
        return remote(
            spot,
            spot,
            wl_send.at[g, s],
            wl_recv.at[g, s],
            left,
        )

    def w_right(g, s):
        spot = wbuf.at[g, dp - 2 * s]
        return remote(
            spot,
            spot,
            wr_send.at[g, s],
            wr_recv.at[g, s],
            right,
        )

    def w_sib(g, o):
        spot = wbuf.at[g, 2 * o + c]
        return remote(spot, spot, ws_send.at[g, o], ws_recv.at[g, o], sibling)

    def w_begin(g):
        @pl.when(has_left)
        def _():
            w_left(g, 0).start()

        @pl.when(has_right)
        def _():
            w_right(g, 0).start()

        w_sib(g, p).start()

    def w_step(g, s):
        @pl.when(p >= s)
        def _():
            spot = wbuf.at[g, dp - 2 * s]
            remote(spot, spot, wr_send.at[g, s], wr_recv.at[g, s - 1], right).wait_recv()

            @pl.when(has_right)
            def _():
                w_right(g, s).start()

            w_sib(g, p - s).start()

        @pl.when(p + s < line)
        def _():
            spot = wbuf.at[g, dp + 2 * s]
            remote(spot, spot, wl_send.at[g, s], wl_recv.at[g, s - 1], left).wait_recv()

            @pl.when(has_left)
            def _():
                w_left(g, s).start()

            w_sib(g, p + s).start()

    def w_finish(g):
        for s in range(line):

            @pl.when(has_left & (p + s < line))
            def _():
                w_left(g, s).wait_send()

            @pl.when(has_right & (p >= s))
            def _():
                w_right(g, s).wait_send()

        for o in range(line):
            w_sib(g, o).wait_send()

    def x_spot(t):
        return xall.at[pl.ds(pl.multiple_of(t * share, 16), share)]

    def x_copy(r):
        return remote(xin, x_spot(ten), x_send.at[r - 1], x_recv.at[r - 1], peer(r))

    def x_wait():
        for r in range(1, t_count):
            x_copy(r).wait_send()
            spot = x_spot(lax.rem(ten + t_count - r, t_count))
            remote(spot, spot, x_send.at[r - 1], x_recv.at[r - 1], peer(r)).wait_recv()
        pltpu.make_async_copy(xin, x_spot(ten), loc_sem.at[groups, 0]).wait()

    def t_copy(r, part):
        spot = pl.ds(part * tile, tile)
        return remote(
            stage.at[r, :, spot],
            tgt.at[r - 1, :, spot],
            t_send.at[r - 1, part],
            t_recv.at[r - 1, part],
            peer(r),
        )

    for copy in own_copies(0):
        copy.wait()
    w_begin(0)
    for g in range(1, groups):
        for copy in own_copies(g):
            copy.wait()
    for r in range(1, t_count):
        x_copy(r).start()
    pltpu.make_async_copy(xin, x_spot(ten), loc_sem.at[groups, 0]).start()

    tiles = t_count * (cols // tile)
    deep = proj.shape[0]

    def tile_spot(i):
        return pl.ds((i % 2) * deep, deep), pl.ds(0, tile)

    def tile_copy(i):
        owner = lax.rem(ten + 1 + i % t_count, t_count)
        return pltpu.make_async_copy(
            proj.at[:, lanes(owner * cols + (i // t_count) * tile, tile)],
            ptile.at[tile_spot(i)],
            tile_sem.at[i % 2],
        )

    tile_copy(0).start()
    tile_copy(1).start()

    def weigh(q, k, first):
        shape = (q.shape[0], k.shape[0])
        visible = lax.broadcasted_iota(jnp.int32, shape, 1) <= first + lax.broadcasted_iota(
            jnp.int32, shape, 0
        )
        scores = jnp.where(visible, dot(q, k, NT) * FACTOR, -1e30)
        shifted = jnp.exp(scores - jnp.max(scores, axis=-1, keepdims=True))
        return shifted, 1.0 / jnp.sum(shifted, axis=-1, keepdims=True)

    half = length // 2 if length % 512 == 0 else length
    blocks = [(first, first + half) for first in range(0, length, half)]

    def teacher_head(h, carry):
        kv = lanes((h // t_ratio) * HEAD)
        spot = lanes(h * HEAD)
        for first, limit in blocks:
            shifted, inverse = weigh(tq[first:limit, spot], tk[:limit, kv], first)
            ctx[first:limit, spot] = (
                dot(shifted.astype(jnp.bfloat16), tv[:limit, kv]) * inverse
            ).astype(jnp.bfloat16)
        return carry

    lax.fori_loop(0, 3 * t_heads // 4, teacher_head, 0)
    w_step(0, 1)
    lax.fori_loop(3 * t_heads // 4, t_heads, teacher_head, 0)
    for i in range(tiles):
        tile_copy(i).wait()
        r = (1 + i) % t_count
        part = i // t_count
        stage[r, :, pl.ds(part * tile, tile)] = dot(ctx[...], ptile[tile_spot(i)]).astype(
            jnp.bfloat16
        )
        if i + 2 < tiles:
            tile_copy(i + 2).start()
        if r:
            t_copy(r, part).start()
    for s in range(2, line - 1):
        w_step(0, s)
    x_wait()

    def x_turned(d):
        return ptile[pl.ds(pl.multiple_of(d * rows, rows), rows), pl.ds(0, length)]

    def turn(d, carry):
        ptile[pl.ds(pl.multiple_of(d * rows, rows), rows), pl.ds(0, length)] = x_cols(d).T
        return carry

    def x_cols(d):
        return xall[:, lanes(d * rows, rows)]

    lax.fori_loop(0, dp_count, turn, 0)

    def absorb(g, begin, end):
        def one(o, carry):
            spot = wbuf.at[g, 2 * o + 1 - c]
            remote(spot, spot, ws_send.at[g, o], ws_recv.at[g, o], sibling).wait_recv()
            acc[...] += dot(x_cols(2 * o), wbuf[g, 2 * o])
            acc[...] += dot(x_cols(2 * o + 1), wbuf[g, 2 * o + 1])
            return carry

        lax.fori_loop(begin, end, one, 0)

    near = jnp.maximum(p - (line - 2), 0)
    far = jnp.minimum(p + (line - 2), line - 1) + 1

    def project(g):
        acc[...] = jnp.zeros_like(acc)
        absorb(g, near, far)
        w_step(g, line - 1)
        if g + 1 < groups:
            w_begin(g + 1)
        absorb(g, 0, near)
        absorb(g, far, line)
        w_finish(g)
        qkv[...] = acc[...].astype(jnp.bfloat16)

    def heads(g, begin, end):
        def one(j, carry):
            lane = lanes(j * HEAD)
            spot = lanes((g * ratio + j) * HEAD)
            for first, limit in blocks:
                q = qkv[first:limit, lane]
                k = qkv[:limit, pl.ds(ratio * HEAD, HEAD)]
                v = qkv[:limit, pl.ds((ratio + 1) * HEAD, HEAD)]
                shifted, inverse = weigh(q, k, first)
                probs = shifted * inverse
                rounded = probs.astype(jnp.bfloat16)
                target = stage[0, first:limit, spot].astype(jnp.float32)
                for r in range(t_count - 1):
                    target += tgt[r, first:limit, spot].astype(jnp.float32)
                incoming = ((dot(rounded, v) - target) / dp_count).astype(jnp.bfloat16)
                gkv[1, :limit] += dot(rounded, incoming, TN)
                grad = dot(incoming, v, NT)
                grad = probs * (grad - jnp.sum(grad * probs, axis=-1, keepdims=True))
                scaled = (grad * FACTOR).astype(jnp.bfloat16)
                grads[first:limit, lane] = dot(scaled, k).astype(jnp.bfloat16)
                gkv[0, :limit] += dot(scaled, q, TN)
            return carry

        lax.fori_loop(begin, end, one, 0)

    def early(g):
        return ratio - 1 if g == groups - 1 else ratio // 2

    def part_cols(q):
        first = early(q // 2) * HEAD
        return pl.ds(first, width - first) if q % 2 else pl.ds(0, first)

    def cut(ref, q, i):
        return ref.at[q // 2, i, :, part_cols(q)]

    def g_sib(q, o):
        return remote(
            cut(wbuf, q, 2 * o + 1 - c),
            cut(sib, q, o),
            gs_send.at[q, o],
            gs_recv.at[q, o],
            sibling,
        )

    def g_right(q, k):
        o = line - 1 - k
        slot = o - p - 1
        return remote(
            cut(wbuf, q, 2 * o + c),
            cut(from_left, q, slot),
            gr_send.at[q, k],
            gr_recv.at[q, slot],
            right,
        )

    def g_left(q, k):
        slot = p - 1 - k
        return remote(
            cut(wbuf, q, 2 * k + c),
            cut(from_right, q, slot),
            gl_send.at[q, k],
            gl_recv.at[q, slot],
            left,
        )

    def wait_left(q, slot):
        spot = cut(from_left, q, slot)
        remote(spot, spot, gr_send.at[q, 0], gr_recv.at[q, slot], right).wait_recv()
        return spot[...].astype(jnp.float32)

    def wait_right(q, slot):
        spot = cut(from_right, q, slot)
        remote(spot, spot, gl_send.at[q, 0], gl_recv.at[q, slot], left).wait_recv()
        return spot[...].astype(jnp.float32)

    def pair(q, o):
        g_sib(q, o).wait_recv()
        return cut(wbuf, q, 2 * o + c)[...].astype(jnp.float32) + cut(sib, q, o)[...].astype(
            jnp.float32
        )

    def products(q):
        if q % 2:
            for j in range(2):
                grads[:, pl.ds((ratio + j) * HEAD, HEAD)] = gkv[j].astype(jnp.bfloat16)
        spot = part_cols(q)

        def one(i, carry):
            o = jnp.where(i % 2 == 0, line - 1 - i // 2, i // 2)
            for core in (1 - c, c):
                d = 2 * o + core
                wbuf[q // 2, d, :, spot] = dot(x_turned(d), grads[:, spot]).astype(jnp.bfloat16)
                if core is not c:
                    g_sib(q, o).start()
            return carry

        lax.fori_loop(0, line, one, 0)

        @pl.when(p == 0)
        def _():
            for k in range(line - 1):
                spot = cut(wbuf, q, 2 * (line - 1 - k) + c)
                spot[...] = pair(q, line - 1 - k).astype(jnp.bfloat16)
                g_right(q, k).start()

        @pl.when(p == line - 1)
        def _():
            for k in range(line - 1):
                spot = cut(wbuf, q, 2 * k + c)
                spot[...] = pair(q, k).astype(jnp.bfloat16)
                g_left(q, k).start()

    def chain(q, k):
        o = line - 1 - k

        @pl.when(has_left & (o > p))
        def _():
            own = pair(q, o)
            spot = cut(wbuf, q, 2 * o + c)
            spot[...] = (own + wait_left(q, o - p)).astype(jnp.bfloat16)
            g_right(q, k).start()

        @pl.when(has_right & (k < p))
        def _():
            own = pair(q, k)
            spot = cut(wbuf, q, 2 * k + c)
            spot[...] = (own + wait_right(q, p - k)).astype(jnp.bfloat16)
            g_left(q, k).start()

    def finish(q):
        total = out.at[q // 2, :, part_cols(q)]
        total[...] = pair(q, p)

        @pl.when(has_left)
        def _():
            total[...] += wait_left(q, 0)

        @pl.when(has_right)
        def _():
            total[...] += wait_right(q, 0)

        for k in range(line - 1):

            @pl.when(line - 1 - k > p)
            def _():
                g_right(q, k).wait_send()

            @pl.when(k < p)
            def _():
                g_left(q, k).wait_send()

        for o in range(line):
            g_sib(q, o).wait_send()

    links = range(line - 2)
    work = []
    for g in range(groups):
        last = g == groups - 1
        project(g)
        gkv[...] = jnp.zeros_like(gkv)
        for part in range(cols // tile):
            if (part * tile) // (ratio * HEAD) == g:
                for r in range(1, t_count):
                    t_copy(r, part).wait()
        for j in range(ratio):
            if j < len(links) and work:
                work.pop(0)()
            heads(g, j, j + 1)
            if j == early(g) - 1:
                products(2 * g)
                if not last:
                    w_step(g + 1, 1)
        if not last:
            for k in links:
                chain(2 * g, k)
        products(2 * g + 1)
        if last:
            for k in links:
                chain(2 * g, k)
        while work:
            work.pop(0)()
        if not last:
            for s in range(2, line - 1):
                w_step(g + 1, s)
        work = [functools.partial(chain, 2 * g + 1, k) for k in links]
        work += [functools.partial(finish, 2 * g), functools.partial(finish, 2 * g + 1)]
    while work:
        work.pop(0)()


def fused_call(tq, tk, tv, projector, xin, query_weight, key_weight, value_weight):
    dp_count = lax.axis_size("dp")
    t_count = lax.axis_size("tensor")
    line = dp_count // 2
    groups = key_weight.shape[1] // HEAD
    rows = query_weight.shape[0]
    q_cols = query_weight.shape[1]
    per = q_cols // groups
    width = per + 2 * HEAD
    length = tq.shape[0]
    cols = projector.shape[1] // t_count
    tile = min(per, cols)
    bf = jnp.bfloat16
    vmem = pl.BlockSpec(memory_space=pltpu.VMEM)
    hbm = pl.BlockSpec(memory_space=pl.ANY)
    sem = pltpu.SemaphoreType.DMA
    out = pl.pallas_call(
        functools.partial(fused, dp_count, t_count),
        out_shape=jax.ShapeDtypeStruct((groups, rows, width), jnp.float32),
        in_specs=[vmem, vmem, vmem] + [hbm] * 5,
        out_specs=vmem,
        scratch_shapes=[
            pltpu.VMEM((groups, dp_count, rows, width), bf),
            pltpu.VMEM((length, xin.shape[1]), bf),
            pltpu.VMEM(tq.shape, bf),
            pltpu.VMEM((max(2 * projector.shape[0], xin.shape[1]), max(tile, length)), bf),
            pltpu.VMEM((t_count, length, cols), bf),
            pltpu.VMEM((t_count - 1, length, cols), bf),
            pltpu.VMEM((groups, line, rows, width), bf),
            pltpu.VMEM((groups, line - 1, rows, width), bf),
            pltpu.VMEM((groups, line - 1, rows, width), bf),
            pltpu.VMEM((length, width), jnp.float32),
            pltpu.VMEM((length, width), bf),
            pltpu.VMEM((length, width), bf),
            pltpu.VMEM((2, length, HEAD), jnp.float32),
            sem((groups + 1, 3)),
            sem((2,)),
            sem((t_count - 1,)),
            sem((t_count - 1,)),
            sem((t_count - 1, cols // tile)),
            sem((t_count - 1, cols // tile)),
        ]
        + [sem((groups, line))] * 6
        + [sem((2 * groups, line))] * 6,
        compiler_params=pltpu.CompilerParams(
            collective_id=0, has_side_effects=True, vmem_limit_bytes=VMEM_LIMIT
        ),
    )(tq, tk, tv, projector, xin, query_weight, key_weight, value_weight)
    return (
        jnp.concatenate([out[g, :, :per] for g in range(groups)], axis=1),
        jnp.concatenate([out[g, :, per : per + HEAD] for g in range(groups)], axis=1),
        jnp.concatenate([out[g, :, per + HEAD :] for g in range(groups)], axis=1),
    )


def per_device(
    teacher_queries,
    teacher_keys,
    teacher_values,
    projector,
    student_inputs,
    query_weight,
    key_weight,
    value_weight,
):
    if teacher_queries.shape[1] <= 512:
        return fused_call(
            teacher_queries[0],
            teacher_keys[0],
            teacher_values[0],
            projector,
            student_inputs[0],
            query_weight,
            key_weight,
            value_weight,
        )
    factor = HEAD ** (-0.5)
    dp_count = lax.axis_size("dp")
    context_t, unused = attend(
        teacher_queries[0], teacher_keys[0], teacher_values[0], TQH // TKVH, factor
    )
    context_t = context_t.astype(jnp.bfloat16)
    summed = lax.psum_scatter(
        lax.dot_general(
            projector, context_t, (((0,), (1,)), ((), ())), preferred_element_type=jnp.float32
        ).astype(jnp.bfloat16),
        "tensor",
        scatter_dimension=0,
        tiled=True,
    ).astype(jnp.float32)
    target = summed.T
    rows_all = lax.all_gather(student_inputs[0], "tensor", axis=0, tiled=True)
    full_weights = (
        lax.all_gather(query_weight, "dp", axis=0, tiled=True),
        lax.all_gather(key_weight, "dp", axis=0, tiled=True),
        lax.all_gather(value_weight, "dp", axis=0, tiled=True),
    )
    rows_all, full_weights = (rows_all, full_weights)
    queries = jnp.dot(rows_all, full_weights[0], preferred_element_type=jnp.float32).astype(
        jnp.bfloat16
    )
    keys = jnp.dot(rows_all, full_weights[1], preferred_element_type=jnp.float32).astype(
        jnp.bfloat16
    )
    values = jnp.dot(rows_all, full_weights[2], preferred_element_type=jnp.float32).astype(
        jnp.bfloat16
    )
    context_s, kept = attend(queries, keys, values, SQH // SKVH, factor)
    grad_context = ((context_s - target) / dp_count).astype(jnp.bfloat16)
    grad_q, grad_k, grad_v = attend_back(
        grad_context, queries, keys, values, kept, SQH // SKVH, factor
    )
    grad_all = jnp.concatenate([grad_q, grad_k, grad_v], axis=1)
    whole = lax.dot_general(
        rows_all, grad_all, (((0,), (0,)), ((), ())), preferred_element_type=jnp.float32
    )
    reduced = lax.psum_scatter(
        whole.astype(jnp.bfloat16), "dp", scatter_dimension=0, tiled=True
    ).astype(jnp.float32)
    query_cols = query_weight.shape[1]
    key_cols = key_weight.shape[1]
    return (
        reduced[:, :query_cols],
        reduced[:, query_cols : query_cols + key_cols],
        reduced[:, query_cols + key_cols :],
    )


def solution(mesh):
    placed = (
        P("dp", None, "tensor"),
        P("dp", None, "tensor"),
        P("dp", None, "tensor"),
        P("tensor", None),
        P("dp", "tensor", None),
        P("dp", "tensor"),
        P("dp", "tensor"),
        P("dp", "tensor"),
    )
    return jax.shard_map(
        per_device,
        mesh=mesh,
        in_specs=placed,
        out_specs=(P("dp", "tensor"), P("dp", "tensor"), P("dp", "tensor")),
        check_vma=False,
    )
```

```python
import functools

import jax
import jax.numpy as jnp
from jax import lax
from jax.experimental import pallas as pl
from jax.experimental.pallas import tpu as pltpu
from jax.sharding import PartitionSpec as P

HEAD = 128
TQH = 64
TKVH = 8
SQH = 32
SKVH = 8
VMEM_LIMIT = 63 * 1024 * 1024


def attend(queries, keys, values, groups, factor):
    length = queries.shape[0]
    heads_kv = keys.shape[1] // HEAD
    query_heads = queries.reshape(length, heads_kv, groups, HEAD)
    key_heads = keys.reshape(length, heads_kv, HEAD)
    value_heads = values.reshape(length, heads_kv, HEAD)
    block_rows = min(512, length)
    pieces = []
    kept = []
    for number in range(length // block_rows):
        first = number * block_rows
        limit = first + block_rows
        scores = (
            jnp.einsum(
                "qhgd,khd->hgqk",
                query_heads[first:limit],
                key_heads[:limit],
                preferred_element_type=jnp.float32,
            )
            * factor
        )
        visible = jnp.arange(limit)[None, :] <= (first + jnp.arange(block_rows))[:, None]
        scores = jnp.where(visible, scores, -1e30)
        shifted = jnp.exp(scores - jnp.max(scores, axis=-1, keepdims=True))
        probs = shifted / jnp.sum(shifted, axis=-1, keepdims=True)
        rounded = probs.astype(jnp.bfloat16)
        context = jnp.einsum(
            "hgqk,khd->qhgd", rounded, value_heads[:limit], preferred_element_type=jnp.float32
        )
        pieces.append(context.reshape(block_rows, -1))
        kept.append(probs)
    return (jnp.concatenate(pieces, axis=0), kept)


def attend_back(incoming_all, queries, keys, values, kept, groups, factor):
    length = queries.shape[0]
    heads_kv = keys.shape[1] // HEAD
    query_heads = queries.reshape(length, heads_kv, groups, HEAD)
    key_heads = keys.reshape(length, heads_kv, HEAD)
    value_heads = values.reshape(length, heads_kv, HEAD)
    block_rows = min(512, length)
    grad_keys = jnp.zeros((length, heads_kv, HEAD), jnp.float32)
    grad_values = jnp.zeros((length, heads_kv, HEAD), jnp.float32)
    query_parts = []
    for number in range(length // block_rows):
        first = number * block_rows
        limit = first + block_rows
        probs = kept[number]
        rounded = probs.astype(jnp.bfloat16)
        incoming = incoming_all[first:limit].reshape(block_rows, heads_kv, groups, HEAD)
        grad_values = grad_values.at[:limit].add(
            jnp.einsum("hgqk,qhgd->khd", rounded, incoming, preferred_element_type=jnp.float32)
        )
        grad_probs = jnp.einsum(
            "qhgd,khd->hgqk", incoming, value_heads[:limit], preferred_element_type=jnp.float32
        )
        grad_scores = probs * (grad_probs - jnp.sum(grad_probs * probs, axis=-1, keepdims=True))
        scaled = (grad_scores * factor).astype(jnp.bfloat16)
        query_parts.append(
            jnp.einsum(
                "hgqk,khd->qhgd", scaled, key_heads[:limit], preferred_element_type=jnp.float32
            ).reshape(block_rows, -1)
        )
        grad_keys = grad_keys.at[:limit].add(
            jnp.einsum(
                "hgqk,qhgd->khd",
                scaled,
                query_heads[first:limit],
                preferred_element_type=jnp.float32,
            )
        )
    grad_queries = jnp.concatenate(query_parts, axis=0).astype(jnp.bfloat16)
    return (
        grad_queries,
        grad_keys.reshape(length, -1).astype(jnp.bfloat16),
        grad_values.reshape(length, -1).astype(jnp.bfloat16),
    )


MESH = pl.DeviceIdType.MESH
FACTOR = HEAD ** (-0.5)
NT = (((1,), (1,)), ((), ()))
TN = (((0,), (0,)), ((), ()))


def dot(a, b, dims=(((1,), (0,)), ((), ()))):
    return lax.dot_general(a, b, dims, preferred_element_type=jnp.float32)


def lanes(start, size=HEAD):
    return pl.ds(pl.multiple_of(start, HEAD), size)


def fused(
    dp_count,
    t_count,
    tq,
    tk,
    tv,
    proj,
    xin,
    qw,
    kw,
    vw,
    out,
    wbuf,
    xall,
    ctx,
    ptile,
    stage,
    tgt,
    sib,
    from_left,
    from_right,
    acc,
    qkv,
    grads,
    gkv,
    loc_sem,
    tile_sem,
    x_send,
    x_recv,
    t_send,
    t_recv,
    wl_send,
    wl_recv,
    wr_send,
    wr_recv,
    ws_send,
    ws_recv,
    gs_send,
    gs_recv,
    gl_send,
    gl_recv,
    gr_send,
    gr_recv,
):
    line = dp_count // 2
    groups = wbuf.shape[0]
    width = wbuf.shape[3]
    rows = wbuf.shape[2]
    length = tq.shape[0]
    share = xin.shape[0]
    ratio = width // HEAD - 2
    t_heads = tq.shape[1] // HEAD
    t_ratio = t_heads // (tk.shape[1] // HEAD)
    cols = stage.shape[2]
    tile = ratio * HEAD
    dp = lax.axis_index("dp")
    ten = lax.axis_index("tensor")
    p = dp // 2
    c = dp % 2
    has_left = p > 0
    has_right = p < line - 1
    left = {"dp": dp - 2}
    right = {"dp": dp + 2}
    sibling = {"dp": dp + 1 - 2 * c}

    def peer(r):
        return {"tensor": lax.rem(ten + r, t_count)}

    def remote(src, dst, send, recv, device):
        return pltpu.make_async_remote_copy(
            src_ref=src,
            dst_ref=dst,
            send_sem=send,
            recv_sem=recv,
            device_id=device,
            device_id_type=MESH,
        )

    def own_copies(g):
        per = ratio * HEAD
        mine = wbuf.at[g, dp]
        return (
            pltpu.make_async_copy(
                qw.at[:, pl.ds(g * per, per)], mine.at[:, pl.ds(0, per)], loc_sem.at[g, 0]
            ),
            pltpu.make_async_copy(
                kw.at[:, pl.ds(g * HEAD, HEAD)], mine.at[:, pl.ds(per, HEAD)], loc_sem.at[g, 1]
            ),
            pltpu.make_async_copy(
                vw.at[:, pl.ds(g * HEAD, HEAD)],
                mine.at[:, pl.ds(per + HEAD, HEAD)],
                loc_sem.at[g, 2],
            ),
        )

    for g in range(groups):
        for copy in own_copies(g):
            copy.start()

    barrier = pltpu.get_barrier_semaphore()

    def hello(device):
        pl.semaphore_signal(barrier, inc=1, device_id=device, device_id_type=MESH)

    @pl.when(has_left)
    def _():
        hello(left)

    @pl.when(has_right)
    def _():
        hello(right)

    hello(sibling)
    for r in range(1, t_count):
        hello(peer(r))
    pl.semaphore_wait(
        barrier, t_count + has_left.astype(jnp.int32) + has_right.astype(jnp.int32)
    )

    def w_left(g, s):
        spot = wbuf.at[g, dp + 2 * s]
        return remote(
            spot,
            spot,
            wl_send.at[g, s],
            wl_recv.at[g, s],
            left,
        )

    def w_right(g, s):
        spot = wbuf.at[g, dp - 2 * s]
        return remote(
            spot,
            spot,
            wr_send.at[g, s],
            wr_recv.at[g, s],
            right,
        )

    def w_sib(g, o):
        spot = wbuf.at[g, 2 * o + c]
        return remote(spot, spot, ws_send.at[g, o], ws_recv.at[g, o], sibling)

    def w_begin(g):
        @pl.when(has_left)
        def _():
            w_left(g, 0).start()

        @pl.when(has_right)
        def _():
            w_right(g, 0).start()

        w_sib(g, p).start()

    def w_step(g, s):
        @pl.when(p >= s)
        def _():
            spot = wbuf.at[g, dp - 2 * s]
            remote(spot, spot, wr_send.at[g, s], wr_recv.at[g, s - 1], right).wait_recv()

            @pl.when(has_right)
            def _():
                w_right(g, s).start()

            w_sib(g, p - s).start()

        @pl.when(p + s < line)
        def _():
            spot = wbuf.at[g, dp + 2 * s]
            remote(spot, spot, wl_send.at[g, s], wl_recv.at[g, s - 1], left).wait_recv()

            @pl.when(has_left)
            def _():
                w_left(g, s).start()

            w_sib(g, p + s).start()

    def w_finish(g):
        for s in range(line):

            @pl.when(has_left & (p + s < line))
            def _():
                w_left(g, s).wait_send()

            @pl.when(has_right & (p >= s))
            def _():
                w_right(g, s).wait_send()

        for o in range(line):
            w_sib(g, o).wait_send()

    def x_spot(t):
        return xall.at[pl.ds(pl.multiple_of(t * share, 16), share)]

    def x_copy(r):
        return remote(xin, x_spot(ten), x_send.at[r - 1], x_recv.at[r - 1], peer(r))

    def x_wait():
        for r in range(1, t_count):
            x_copy(r).wait_send()
            spot = x_spot(lax.rem(ten + t_count - r, t_count))
            remote(spot, spot, x_send.at[r - 1], x_recv.at[r - 1], peer(r)).wait_recv()
        pltpu.make_async_copy(xin, x_spot(ten), loc_sem.at[groups, 0]).wait()

    def t_copy(r, part):
        spot = pl.ds(part * tile, tile)
        return remote(
            stage.at[r, :, spot],
            tgt.at[r - 1, :, spot],
            t_send.at[r - 1, part],
            t_recv.at[r - 1, part],
            peer(r),
        )

    for copy in own_copies(0):
        copy.wait()
    w_begin(0)
    for g in range(1, groups):
        for copy in own_copies(g):
            copy.wait()
    for r in range(1, t_count):
        x_copy(r).start()
    pltpu.make_async_copy(xin, x_spot(ten), loc_sem.at[groups, 0]).start()

    tiles = t_count * (cols // tile)
    deep = proj.shape[0]

    def tile_spot(i):
        return pl.ds((i % 2) * deep, deep), pl.ds(0, tile)

    def tile_copy(i):
        owner = lax.rem(ten + 1 + i % t_count, t_count)
        return pltpu.make_async_copy(
            proj.at[:, lanes(owner * cols + (i // t_count) * tile, tile)],
            ptile.at[tile_spot(i)],
            tile_sem.at[i % 2],
        )

    tile_copy(0).start()
    tile_copy(1).start()

    def weigh(q, k, first):
        shape = (q.shape[0], k.shape[0])
        visible = lax.broadcasted_iota(jnp.int32, shape, 1) <= first + lax.broadcasted_iota(
            jnp.int32, shape, 0
        )
        scores = jnp.where(visible, dot(q, k, NT) * FACTOR, -1e30)
        shifted = jnp.exp(scores - jnp.max(scores, axis=-1, keepdims=True))
        return shifted, 1.0 / jnp.sum(shifted, axis=-1, keepdims=True)

    half = length // 2 if length % 512 == 0 else length
    blocks = [(first, first + half) for first in range(0, length, half)]

    def teacher_head(h, carry):
        kv = lanes((h // t_ratio) * HEAD)
        spot = lanes(h * HEAD)
        for first, limit in blocks:
            shifted, inverse = weigh(tq[first:limit, spot], tk[:limit, kv], first)
            ctx[first:limit, spot] = (
                dot(shifted.astype(jnp.bfloat16), tv[:limit, kv]) * inverse
            ).astype(jnp.bfloat16)
        return carry

    lax.fori_loop(0, 3 * t_heads // 4, teacher_head, 0, unroll=2)
    w_step(0, 1)
    lax.fori_loop(3 * t_heads // 4, t_heads, teacher_head, 0, unroll=2)
    for i in range(tiles):
        tile_copy(i).wait()
        r = (1 + i) % t_count
        part = i // t_count
        stage[r, :, pl.ds(part * tile, tile)] = dot(ctx[...], ptile[tile_spot(i)]).astype(
            jnp.bfloat16
        )
        if i + 2 < tiles:
            tile_copy(i + 2).start()
        if r and part == 0:
            t_copy(r, part).start()
    for s in range(2, line - 1):
        w_step(0, s)
    x_wait()

    def x_turned(d):
        return ptile[pl.ds(pl.multiple_of(d * rows, rows), rows), pl.ds(0, length)]

    def turn(d, carry):
        ptile[pl.ds(pl.multiple_of(d * rows, rows), rows), pl.ds(0, length)] = x_cols(d).T
        return carry

    def x_cols(d):
        return xall[:, lanes(d * rows, rows)]

    lax.fori_loop(0, dp_count, turn, 0)

    def absorb(g, begin, end):
        def one(o, carry):
            spot = wbuf.at[g, 2 * o + 1 - c]
            remote(spot, spot, ws_send.at[g, o], ws_recv.at[g, o], sibling).wait_recv()
            acc[...] += dot(x_cols(2 * o), wbuf[g, 2 * o])
            acc[...] += dot(x_cols(2 * o + 1), wbuf[g, 2 * o + 1])
            return carry

        lax.fori_loop(begin, end, one, 0)

    near = jnp.maximum(p - (line - 2), 0)
    far = jnp.minimum(p + (line - 2), line - 1) + 1

    def project(g):
        acc[...] = jnp.zeros_like(acc)
        absorb(g, near, far)
        w_step(g, line - 1)
        if g + 1 < groups:
            w_begin(g + 1)
        absorb(g, 0, near)
        absorb(g, far, line)
        w_finish(g)
        qkv[...] = acc[...].astype(jnp.bfloat16)

    def heads(g, begin, end):
        def one(j, carry):
            lane = lanes(j * HEAD)
            spot = lanes((g * ratio + j) * HEAD)
            for first, limit in blocks:
                q = qkv[first:limit, lane]
                k = qkv[:limit, pl.ds(ratio * HEAD, HEAD)]
                v = qkv[:limit, pl.ds((ratio + 1) * HEAD, HEAD)]
                shifted, inverse = weigh(q, k, first)
                probs = shifted * inverse
                rounded = probs.astype(jnp.bfloat16)
                target = stage[0, first:limit, spot].astype(jnp.float32)
                for r in range(t_count - 1):
                    target += tgt[r, first:limit, spot].astype(jnp.float32)
                incoming = ((dot(rounded, v) - target) / dp_count).astype(jnp.bfloat16)
                gkv[1, :limit] += dot(rounded, incoming, TN)
                grad = dot(incoming, v, NT)
                grad = probs * (grad - jnp.sum(grad * probs, axis=-1, keepdims=True))
                scaled = (grad * FACTOR).astype(jnp.bfloat16)
                grads[first:limit, lane] = dot(scaled, k).astype(jnp.bfloat16)
                gkv[0, :limit] += dot(scaled, q, TN)
            return carry

        lax.fori_loop(begin, end, one, 0)

    def early(g):
        return ratio - 1 if g == groups - 1 else ratio // 2

    def part_cols(q):
        first = early(q // 2) * HEAD
        return pl.ds(first, width - first) if q % 2 else pl.ds(0, first)

    def cut(ref, q, i):
        return ref.at[q // 2, i, :, part_cols(q)]

    def g_sib(q, o):
        return remote(
            cut(wbuf, q, 2 * o + 1 - c),
            cut(sib, q, o),
            gs_send.at[q, o],
            gs_recv.at[q, o],
            sibling,
        )

    def g_right(q, k):
        o = line - 1 - k
        slot = o - p - 1
        return remote(
            cut(wbuf, q, 2 * o + c),
            cut(from_left, q, slot),
            gr_send.at[q, k],
            gr_recv.at[q, slot],
            right,
        )

    def g_left(q, k):
        slot = p - 1 - k
        return remote(
            cut(wbuf, q, 2 * k + c),
            cut(from_right, q, slot),
            gl_send.at[q, k],
            gl_recv.at[q, slot],
            left,
        )

    def wait_left(q, slot):
        spot = cut(from_left, q, slot)
        remote(spot, spot, gr_send.at[q, 0], gr_recv.at[q, slot], right).wait_recv()
        return spot[...].astype(jnp.float32)

    def wait_right(q, slot):
        spot = cut(from_right, q, slot)
        remote(spot, spot, gl_send.at[q, 0], gl_recv.at[q, slot], left).wait_recv()
        return spot[...].astype(jnp.float32)

    def pair(q, o):
        g_sib(q, o).wait_recv()
        return cut(wbuf, q, 2 * o + c)[...].astype(jnp.float32) + cut(sib, q, o)[...].astype(
            jnp.float32
        )

    def products(q):
        if q % 2:
            for j in range(2):
                grads[:, pl.ds((ratio + j) * HEAD, HEAD)] = gkv[j].astype(jnp.bfloat16)
        spot = part_cols(q)

        def one(i, carry):
            o = jnp.where(i % 2 == 0, line - 1 - i // 2, i // 2)
            for core in (1 - c, c):
                d = 2 * o + core
                wbuf[q // 2, d, :, spot] = dot(x_turned(d), grads[:, spot]).astype(jnp.bfloat16)
                if core is not c:
                    g_sib(q, o).start()
            return carry

        lax.fori_loop(0, line, one, 0)

        @pl.when(p == 0)
        def _():
            for k in range(line - 1):
                spot = cut(wbuf, q, 2 * (line - 1 - k) + c)
                spot[...] = pair(q, line - 1 - k).astype(jnp.bfloat16)
                g_right(q, k).start()

        @pl.when(p == line - 1)
        def _():
            for k in range(line - 1):
                spot = cut(wbuf, q, 2 * k + c)
                spot[...] = pair(q, k).astype(jnp.bfloat16)
                g_left(q, k).start()

    def chain(q, k):
        o = line - 1 - k

        @pl.when(has_left & (o > p))
        def _():
            own = pair(q, o)
            spot = cut(wbuf, q, 2 * o + c)
            spot[...] = (own + wait_left(q, o - p)).astype(jnp.bfloat16)
            g_right(q, k).start()

        @pl.when(has_right & (k < p))
        def _():
            own = pair(q, k)
            spot = cut(wbuf, q, 2 * k + c)
            spot[...] = (own + wait_right(q, p - k)).astype(jnp.bfloat16)
            g_left(q, k).start()

    def finish(q):
        total = out.at[q // 2, :, part_cols(q)]
        total[...] = pair(q, p)

        @pl.when(has_left)
        def _():
            total[...] += wait_left(q, 0)

        @pl.when(has_right)
        def _():
            total[...] += wait_right(q, 0)

        for k in range(line - 1):

            @pl.when(line - 1 - k > p)
            def _():
                g_right(q, k).wait_send()

            @pl.when(k < p)
            def _():
                g_left(q, k).wait_send()

        for o in range(line):
            g_sib(q, o).wait_send()

    links = range(line - 2)
    work = []
    for g in range(groups):
        last = g == groups - 1
        project(g)
        gkv[...] = jnp.zeros_like(gkv)
        for part in range(cols // tile):
            if (part * tile) // (ratio * HEAD) == g:
                for r in range(1, t_count):
                    t_copy(r, part).wait()
                if part + 1 < cols // tile:
                    for r in range(1, t_count):
                        t_copy(r, part + 1).start()
        for j in range(ratio):
            if j < len(links) and work:
                work.pop(0)()
            heads(g, j, j + 1)
            if j == early(g) - 1:
                products(2 * g)
                if not last:
                    w_step(g + 1, 1)
        if not last:
            for k in links:
                chain(2 * g, k)
        products(2 * g + 1)
        if last:
            for k in links:
                chain(2 * g, k)
        while work:
            work.pop(0)()
        if not last:
            for s in range(2, line - 1):
                w_step(g + 1, s)
        work = [functools.partial(chain, 2 * g + 1, k) for k in links]
        work += [functools.partial(finish, 2 * g), functools.partial(finish, 2 * g + 1)]
    while work:
        work.pop(0)()


def fused_call(tq, tk, tv, projector, xin, query_weight, key_weight, value_weight):
    dp_count = lax.axis_size("dp")
    t_count = lax.axis_size("tensor")
    line = dp_count // 2
    groups = key_weight.shape[1] // HEAD
    rows = query_weight.shape[0]
    q_cols = query_weight.shape[1]
    per = q_cols // groups
    width = per + 2 * HEAD
    length = tq.shape[0]
    cols = projector.shape[1] // t_count
    tile = min(per, cols)
    bf = jnp.bfloat16
    vmem = pl.BlockSpec(memory_space=pltpu.VMEM)
    hbm = pl.BlockSpec(memory_space=pl.ANY)
    sem = pltpu.SemaphoreType.DMA
    out = pl.pallas_call(
        functools.partial(fused, dp_count, t_count),
        out_shape=jax.ShapeDtypeStruct((groups, rows, width), jnp.float32),
        in_specs=[vmem, vmem, vmem] + [hbm] * 5,
        out_specs=vmem,
        scratch_shapes=[
            pltpu.VMEM((groups, dp_count, rows, width), bf),
            pltpu.VMEM((length, xin.shape[1]), bf),
            pltpu.VMEM(tq.shape, bf),
            pltpu.VMEM((max(2 * projector.shape[0], xin.shape[1]), max(tile, length)), bf),
            pltpu.VMEM((t_count, length, cols), bf),
            pltpu.VMEM((t_count - 1, length, cols), bf),
            pltpu.VMEM((groups, line, rows, width), bf),
            pltpu.VMEM((groups, line - 1, rows, width), bf),
            pltpu.VMEM((groups, line - 1, rows, width), bf),
            pltpu.VMEM((length, width), jnp.float32),
            pltpu.VMEM((length, width), bf),
            pltpu.VMEM((length, width), bf),
            pltpu.VMEM((2, length, HEAD), jnp.float32),
            sem((groups + 1, 3)),
            sem((2,)),
            sem((t_count - 1,)),
            sem((t_count - 1,)),
            sem((t_count - 1, cols // tile)),
            sem((t_count - 1, cols // tile)),
        ]
        + [sem((groups, line))] * 6
        + [sem((2 * groups, line))] * 6,
        compiler_params=pltpu.CompilerParams(
            collective_id=0, has_side_effects=True, vmem_limit_bytes=VMEM_LIMIT
        ),
    )(tq, tk, tv, projector, xin, query_weight, key_weight, value_weight)
    return (
        jnp.concatenate([out[g, :, :per] for g in range(groups)], axis=1),
        jnp.concatenate([out[g, :, per : per + HEAD] for g in range(groups)], axis=1),
        jnp.concatenate([out[g, :, per + HEAD :] for g in range(groups)], axis=1),
    )


def per_device(
    teacher_queries,
    teacher_keys,
    teacher_values,
    projector,
    student_inputs,
    query_weight,
    key_weight,
    value_weight,
):
    if teacher_queries.shape[1] <= 512:
        return fused_call(
            teacher_queries[0],
            teacher_keys[0],
            teacher_values[0],
            projector,
            student_inputs[0],
            query_weight,
            key_weight,
            value_weight,
        )
    factor = HEAD ** (-0.5)
    dp_count = lax.axis_size("dp")
    context_t, unused = attend(
        teacher_queries[0], teacher_keys[0], teacher_values[0], TQH // TKVH, factor
    )
    context_t = context_t.astype(jnp.bfloat16)
    summed = lax.psum_scatter(
        lax.dot_general(
            projector, context_t, (((0,), (1,)), ((), ())), preferred_element_type=jnp.float32
        ).astype(jnp.bfloat16),
        "tensor",
        scatter_dimension=0,
        tiled=True,
    ).astype(jnp.float32)
    target = summed.T
    rows_all = lax.all_gather(student_inputs[0], "tensor", axis=0, tiled=True)
    full_weights = (
        lax.all_gather(query_weight, "dp", axis=0, tiled=True),
        lax.all_gather(key_weight, "dp", axis=0, tiled=True),
        lax.all_gather(value_weight, "dp", axis=0, tiled=True),
    )
    rows_all, full_weights = (rows_all, full_weights)
    queries = jnp.dot(rows_all, full_weights[0], preferred_element_type=jnp.float32).astype(
        jnp.bfloat16
    )
    keys = jnp.dot(rows_all, full_weights[1], preferred_element_type=jnp.float32).astype(
        jnp.bfloat16
    )
    values = jnp.dot(rows_all, full_weights[2], preferred_element_type=jnp.float32).astype(
        jnp.bfloat16
    )
    context_s, kept = attend(queries, keys, values, SQH // SKVH, factor)
    grad_context = ((context_s - target) / dp_count).astype(jnp.bfloat16)
    grad_q, grad_k, grad_v = attend_back(
        grad_context, queries, keys, values, kept, SQH // SKVH, factor
    )
    grad_all = jnp.concatenate([grad_q, grad_k, grad_v], axis=1)
    whole = lax.dot_general(
        rows_all, grad_all, (((0,), (0,)), ((), ())), preferred_element_type=jnp.float32
    )
    reduced = lax.psum_scatter(
        whole.astype(jnp.bfloat16), "dp", scatter_dimension=0, tiled=True
    ).astype(jnp.float32)
    query_cols = query_weight.shape[1]
    key_cols = key_weight.shape[1]
    return (
        reduced[:, :query_cols],
        reduced[:, query_cols : query_cols + key_cols],
        reduced[:, query_cols + key_cols :],
    )


def solution(mesh):
    placed = (
        P("dp", None, "tensor"),
        P("dp", None, "tensor"),
        P("dp", None, "tensor"),
        P("tensor", None),
        P("dp", "tensor", None),
        P("dp", "tensor"),
        P("dp", "tensor"),
        P("dp", "tensor"),
    )
    return jax.shard_map(
        per_device,
        mesh=mesh,
        in_specs=placed,
        out_specs=(P("dp", "tensor"), P("dp", "tensor"), P("dp", "tensor")),
        check_vma=False,
    )
```
